128 devices in a mesh: wide: 16 (over x, y), sub: 8 (over z, core).
Axes of the slice: x: 4, y: 4, z: 4, core: 2. Of those that a mesh axis runs over, the one named last changes fastest.
Arguments:
- krylov_basis: float32 [4, 16384, 16, 128], P(None, ('wide', 'sub')), may hold values from -5 to 5
- quad_weight: float32 [16384, 128], P(('wide', 'sub')), may hold values from 0.5 to 18
- corrections: bfloat16 [16384, 3, 128, 128], P(('wide', 'sub')), may hold values from -0.3125 to 0.3125
- patch_route: int32 [16384, 1], P(('wide', 'sub')), may hold values from 0 to 7; in each aligned block of 128 rows (0 to 127, 128 to 255, ...) at most 64 rows name the same one
- leaf_slot: int32 [16384], P(('wide', 'sub')), may hold values from 0 to 7
- multipole_map: bfloat16 [128, 256], replicated, may hold values from -0.5 to 0.5
- upward_translation: float32 [1024, 256, 256], P(('wide', 'sub')), may hold values from -0.375 to 0.375
- far_coupling: float32 [16, 16, 256, 256], P('wide', None, 'sub'), may hold values from -0.09375 to 0.09375
- downward_translation: float32 [1024, 256, 256], P(('wide', 'sub')), may hold values from -0.375 to 0.375
- evaluation_map: bfloat16 [256, 128], replicated, may hold values from -0.375 to 0.375
Outputs:
- new_vector: float32 [16384, 16, 128], P(('wide', 'sub'))
- hessenberg: float32 [5, 16], replicated
The draws below stay inside these ranges and needn't reach their ends.
Inputs may be any that keep to these rules, and one draw needn't show every extreme that they name: `patch_route`: within each aligned block of the 128 patches of one device, at most 64 patches share a value.
All inputs are finite; a program needn't handle non-finite values.
Results may differ from the reference program's by a relative error of at most 0.004.
Values may be sent and summed in bfloat16 or wider, within the bound.
A program may use at most 128 MiB of HBM per device.

```python
import math
import jax
import jax.numpy as jnp
import numpy as np
from jax import lax

Q = 128
K = 256
R = 16
J = 4
LEAF_DEV = 8
PATCH_DEV = 128
CAP = 64
SUBTREES = 16
SUBTREE = 1024
NPATCH = 16384
NLEAF = 1024
NNODES = 2097152
N_SUB = 8


def draw_quad_weight(key, part):
    key = jax.random.fold_in(key, 11)
    patch_pos = jnp.arange(NPATCH, dtype=jnp.float32)[:, None] / (NPATCH - 1)
    base_values = jnp.exp(jax.random.uniform(key, (NPATCH, Q), jnp.float32, math.log(0.5), math.log(2.0)))
    return base_values * (1.0 + 2.0 * patch_pos)


def draw_krylov_basis(key, part):
    key = jax.random.fold_in(key, 23)
    common_key = jax.random.fold_in(key, 1)
    single_key = jax.random.fold_in(key, 2)
    common_part = jnp.clip(jax.random.normal(common_key, (1, NPATCH, R, Q), jnp.float32), -4.0, 4.0)
    single_part = jnp.clip(jax.random.normal(single_key, (J, NPATCH, R, Q), jnp.float32), -4.0, 4.0)
    return jnp.clip(0.4 * common_part + 0.9165 * single_part, -5.0, 5.0)


def with_ends(array, stream_key, smallest, top_value):
    extent = array.shape
    spot = [jax.random.randint(jax.random.fold_in(stream_key, axis), (), 0, extent[axis]) for axis in range(len(extent))]
    array = array.at[tuple(spot)].set(smallest)
    longest = extent.index(max(extent))
    spot[longest] = (spot[longest] + 1) % extent[longest]
    return array.at[tuple(spot)].set(top_value)


def block_scale(stream_key, shape, cuts, smallest, high):
    def one(position, parts):
        draws = jax.random.uniform(jax.random.fold_in(jax.random.fold_in(stream_key, 6), position), (parts,), jnp.float32, smallest / len(cuts), high / len(cuts))
        return jnp.repeat(jnp.exp(draws), shape[position] // parts).reshape((-1,) + (1,) * (len(shape) - position - 1))

    factor_of = one(*cuts[0])
    for cut in cuts[1:]:
        factor_of = factor_of * one(*cut)
    return factor_of


def deal_out(key, own, number, rows, amount, top, limit, skew):
    sequence = jax.random.permutation(key, amount)
    packed, usual = shares(amount, rows * top, limit, skew, True), shares(amount, rows * top, limit, skew, False)
    places = jnp.arange(amount)

    def named(sizes, offset_by):
        used = int((sizes > 0).sum())
        fixed = max(1, used // 4)
        moved = fixed + (places - fixed + offset_by * (used - fixed)) % max(1, amount - fixed)
        return jnp.zeros((amount,), jnp.int32).at[sequence[jnp.where(places < fixed, places, moved)]].set(jnp.asarray(sizes, jnp.int32))

    sizes = jnp.where(number % 4 == 0, named(packed, number // 4), named(usual, number - number // 4 - 1))
    mixed = jax.random.permutation(jax.random.fold_in(own, 3), amount)
    source_of, receiver = mixed[0:amount // 2 * 2:2], mixed[1:amount // 2 * 2:2]
    room = jnp.minimum(sizes[source_of] - 1, limit - sizes[receiver]) // 2
    room = jnp.where((source_of == sequence[0]) | (receiver == sequence[0]) | (sizes[receiver] == 0), 0, jnp.maximum(room, 0))
    moved = jax.random.randint(jax.random.fold_in(own, 4), (amount // 2,), 0, 1 << 20) % (room + 1)
    sizes = sizes.at[source_of].add(-moved).at[receiver].add(moved)
    items = jnp.searchsorted(jnp.cumsum(sizes), jnp.arange(rows * top), side="right").astype(jnp.int32)
    listing = items.reshape(top, rows).T
    listing = listing[jax.random.permutation(jax.random.fold_in(own, 1), rows)]
    offset_by = jax.random.randint(jax.random.fold_in(own, 2), (rows, 1), 0, top)
    return jnp.take_along_axis(listing, (jnp.arange(top)[None, :] + offset_by) % top, axis=1)


def shares(amount, total, limit, slope, full):
    loads = [(1 << 20) // math.isqrt(grade ** slope) + 1 for grade in range(1, amount + 1)]
    largest = limit if full else min(limit, max(-(-total // amount), total * loads[0] // sum(loads)))
    least = 1 if total - largest >= amount - 1 else 0
    given, surplus = [largest] + [least] * (amount - 1), total - largest - least * (amount - 1)
    while surplus > 0:
        free = [i for i in range(1, amount) if given[i] < largest] or [i for i in range(1, amount) if given[i] < limit]
        mass, budget = sum([loads[i] for i in free]), surplus
        for i in free:
            addition = min(limit - given[i], max(1, budget * loads[i] // mass), surplus)
            given[i] = given[i] + addition
            surplus = surplus - addition
    return np.array(given)


def bell_draw(key, extent, width, reach, split=(), kind=jnp.bfloat16):
    level = block_scale(key, extent, split, -0.22, 0.18) if split else 1.0
    array = jax.random.normal(key, extent, jnp.float32) * width * level
    return jnp.minimum(jnp.maximum(array, -reach), reach).astype(kind)


def setup_inputs(seed: int = 0) -> dict:
    key_of = jax.random.split(jax.random.key(seed), 11)
    krylov_basis = draw_krylov_basis(jax.random.fold_in(key_of[10], 71), 0)
    quad_weight = draw_quad_weight(jax.random.fold_in(key_of[10], 71), 0)
    corrections = bell_draw(key_of[2], (NPATCH, 3, Q, Q), (3 * Q) ** -0.5, 0.3125, ((0, 128),))
    patch_route_keys = jax.random.split(jax.random.fold_in(key_of[3], 1), NPATCH // PATCH_DEV)
    patch_route_turns = jax.random.permutation(jax.random.fold_in(key_of[3], 3), NPATCH // PATCH_DEV)
    patch_route = jax.vmap(lambda own, number: deal_out(jax.random.fold_in(key_of[3], 2), own, number, PATCH_DEV, N_SUB, 1, CAP, 2))(patch_route_keys, patch_route_turns).reshape((NPATCH, 1))
    leaf_slot = with_ends(jax.random.randint(key_of[4], (NPATCH,), 0, LEAF_DEV), jax.random.fold_in(key_of[4], 1), 0, LEAF_DEV - 1).astype(jnp.int32)
    multipole_map = bell_draw(key_of[5], (Q, K), Q ** -0.5, 0.5)
    upward_translation = bell_draw(key_of[6], (NLEAF, K, K), K ** -0.5, 0.375, ((0, 128),), jnp.float32)
    far_coupling = bell_draw(key_of[7], (SUBTREES, SUBTREES, K, K), (SUBTREES * K) ** -0.5, 0.09375, ((0, 16), (2, 8)), jnp.float32)
    downward_translation = bell_draw(key_of[8], (NLEAF, K, K), K ** -0.5, 0.375, ((0, 128),), jnp.float32)
    evaluation_map = bell_draw(key_of[9], (K, Q), K ** -0.5, 0.375)
    return {"krylov_basis": krylov_basis, "quad_weight": quad_weight, "corrections": corrections, "patch_route": patch_route, "leaf_slot": leaf_slot, "multipole_map": multipole_map, "upward_translation": upward_translation, "far_coupling": far_coupling, "downward_translation": downward_translation, "evaluation_map": evaluation_map}


def block_parts(operands):
    vectors, blocks = operands
    return jnp.einsum('pra,pjab->pjrb', vectors.astype(jnp.float32), blocks.astype(jnp.float32))

def weighted_products(basis_set, vector, weights):
    return jnp.einsum('jprq,prq,pq->jr', basis_set, vector, weights, precision=lax.Precision.HIGHEST) / NNODES

def weighted_square(vector, weights):
    return jnp.einsum('prq,prq,pq->r', vector, vector, weights, precision=lax.Precision.HIGHEST) / NNODES

def upward_block(operands):
    block_moments, block_up = operands
    return jnp.einsum('lrk,lkc->rc', block_moments, block_up, precision=lax.Precision.HIGHEST)

def reference(krylov_basis, quad_weight, corrections, patch_route, leaf_slot, multipole_map, upward_translation, far_coupling, downward_translation, evaluation_map):
    current = krylov_basis[J - 1]
    current_half = current.astype(jnp.bfloat16)
    groups = NPATCH // PATCH_DEV
    partials = lax.map(block_parts, (current_half.reshape(groups, PATCH_DEV, R, Q), corrections.reshape(groups, PATCH_DEV, 3, Q, Q)))
    partials = partials.reshape(NPATCH, 3, R, Q)
    zero_row = jnp.zeros((1, R, Q), jnp.float32)
    near_field = partials[:, 1] + jnp.concatenate([partials[1:, 0], zero_row], axis=0) + jnp.concatenate([zero_row, partials[:-1, 2]], axis=0)
    weighted = (current * quad_weight[:, None, :] * (1.0 / math.sqrt(SUBTREE))).astype(jnp.bfloat16)
    patch_ids = jnp.arange(NPATCH, dtype=jnp.int32)
    leaf_of = (patch_ids // SUBTREE * N_SUB + patch_route[:, 0].astype(jnp.int32)) * LEAF_DEV + leaf_slot.astype(jnp.int32)
    expanded = jnp.einsum('prq,qk->prk', weighted.astype(jnp.float32), multipole_map.astype(jnp.float32))
    moments = jax.ops.segment_sum(expanded, leaf_of, num_segments=NLEAF)
    group_leaves = N_SUB * LEAF_DEV
    trees = lax.map(upward_block, (moments.reshape(SUBTREES, group_leaves, R, K), upward_translation.reshape(SUBTREES, group_leaves, K, K)))
    local_exp = jnp.einsum('vrk,wvkc->wrc', trees, far_coupling, precision=lax.Precision.HIGHEST)

    def downward_one(operands):
        tree_local, block_down = operands
        terms = jnp.einsum('rk,lkc->lrc', tree_local, block_down, precision=lax.Precision.HIGHEST).astype(jnp.bfloat16)
        return jnp.einsum('lrk,kq->lrq', terms.astype(jnp.float32), evaluation_map.astype(jnp.float32)).astype(jnp.bfloat16)
    leaf_field = lax.map(downward_one, (local_exp, downward_translation.reshape(SUBTREES, group_leaves, K, K))).reshape(NLEAF, R, Q)
    far_field = lax.optimization_barrier(leaf_field[leaf_of]).astype(jnp.float32)
    image = 0.5 * current + near_field + far_field
    first_coeffs = weighted_products(krylov_basis, image, quad_weight)
    after_first = image - jnp.einsum('jr,jprq->prq', first_coeffs, krylov_basis, precision=lax.Precision.HIGHEST)
    second_coeffs = weighted_products(krylov_basis, after_first, quad_weight)
    remainder = after_first - jnp.einsum('jr,jprq->prq', second_coeffs, krylov_basis, precision=lax.Precision.HIGHEST)
    beta_norm = jnp.sqrt(weighted_square(remainder, quad_weight) + 1e-06)
    new_vector = remainder / beta_norm[None, :, None]
    hessenberg = jnp.concatenate([first_coeffs + second_coeffs, beta_norm[None]], axis=0)
    return (new_vector, hessenberg)
```

```python
import functools

import jax
import jax.numpy as jnp
from jax import lax
from jax.experimental import pallas as pl
from jax.experimental.pallas import tpu as pltpu
from jax.sharding import PartitionSpec as P

MESH = pl.DeviceIdType.MESH
F32 = jnp.float32
BF16 = jnp.bfloat16
WIDE, SUB = 16, 8
PATCHES, RHS, NODES, COEFFS, BASIS, LEAVES = 128, 16, 128, 256, 4, 8
SHARE = COEFFS // SUB
ROWS = PATCHES * RHS
TOTAL = float(WIDE * SUB * PATCHES * NODES)
SCALE = 1.0 / 32.0
PAIRS = [(j, k) for j in range(BASIS) for k in range(j, BASIS)]
NEAR_CHUNKS = 4


def split(value):
    high = value.astype(BF16)
    return high, (value - high.astype(F32)).astype(BF16)


def dot(a, b):
    return jnp.dot(a, b, preferred_element_type=F32)


def split_dot(value, high_ref, low_ref):
    high, low = split(value)
    rows = value.shape[0]
    both = dot(jnp.concatenate([high, low], axis=0), high_ref[...])
    return both[:rows] + both[rows:] + dot(high, low_ref[...])


def patch_rows(p):
    return pl.ds(pl.multiple_of(p * RHS, RHS), RHS)


def kernel(
    basis_hbm, weight_hbm, corr_hbm, route_hbm, slot_hbm, multi_hbm, up_hbm, far_hbm, down_hbm,
    eval_hbm, vector_out, hess_out,
    basis, weight, corr, route_v, slot_v, route_s, slot_s, multi, up, far, down, evalm, edge_corr,
    up_high, up_low, far_high, far_low, down_high, down_low, image,
    send1, recv1, sums1, send2, recv2, send3, recv3, send4, recv4, field,
    edge_send, edge_recv, send6, recv6, send7, recv7,
    load_sem, corr_sem, edge_s, edge_r, s1, r1, s2, r2, s3, r3, s4, r4, s5, r5, s6, r6, s7, r7,
):
    w = lax.axis_index("wide")
    s = lax.axis_index("sub")
    me = w * SUB + s
    below = lax.rem(me + WIDE * SUB - 1, WIDE * SUB)
    above = lax.rem(me + 1, WIDE * SUB)
    below_id = (below // SUB, lax.rem(below, SUB))
    above_id = (above // SUB, lax.rem(above, SUB))
    subs = [lax.rem(s + d, SUB) for d in range(1, SUB)]
    wides = [lax.rem(w + d, WIDE) for d in range(1, WIDE)]
    wide_sources = [lax.rem(w + WIDE - d, WIDE) for d in range(1, WIDE)]

    barrier = pltpu.get_barrier_semaphore()
    peers = [(w, t) for t in subs] + [(v, s) for v in wides] + [below_id, above_id]
    for peer in peers:
        pl.semaphore_signal(barrier, inc=1, device_id=peer, device_id_type=MESH)

    last = BASIS - 1
    loads = {}

    def load(name, source, target):
        copy = pltpu.make_async_copy(source, target, load_sem.at[len(loads)])
        copy.start()
        loads[name] = copy

    load("current", basis_hbm.at[last], basis.at[last])
    load("weight", weight_hbm, weight)
    load("route_v", route_hbm, route_v)
    load("slot_v", slot_hbm, slot_v)
    load("multi", multi_hbm, multi)
    load("up", up_hbm, up)
    load("edge0", corr_hbm.at[0], edge_corr.at[0])
    load("edge1", corr_hbm.at[3 * PATCHES - 1], edge_corr.at[1])
    load("route_s", route_hbm, route_s)
    load("slot_s", slot_hbm, slot_s)
    load("far", far_hbm, far)
    load("eval", eval_hbm, evalm)
    load("down", down_hbm, down)
    blocks = 3 * PATCHES // NEAR_CHUNKS
    corr_loads = []
    for c in range(NEAR_CHUNKS):
        copy = pltpu.make_async_copy(
            corr_hbm.at[pl.ds(c * blocks, blocks)], corr.at[pl.ds(c * blocks, blocks)], corr_sem.at[c]
        )
        copy.start()
        corr_loads.append(copy)
    for j in range(last):
        load("basis%d" % j, basis_hbm.at[j], basis.at[j])

    def start_all(copies):
        for copy in copies:
            copy.start()
        return copies

    def remote(source, target, send_sem, recv_sem, device):
        return pltpu.make_async_remote_copy(
            src_ref=source, dst_ref=target, send_sem=send_sem, recv_sem=recv_sem,
            device_id=device, device_id_type=MESH,
        )

    for name in ("current", "weight", "route_v", "slot_v"):
        loads[name].wait()
    leaf_row = route_v[...] * LEAVES + slot_v[...]
    leaf_count = SUB * LEAVES
    hot = (
        lax.broadcasted_iota(jnp.int32, (leaf_count, PATCHES), 0)
        == jnp.broadcast_to(leaf_row, (leaf_count, PATCHES))
    ).astype(F32).astype(BF16)
    scaled_weight = weight[...] * SCALE
    for r in range(0, RHS, 2):
        pair = [
            (basis[last, pl.ds(r + i, PATCHES, stride=RHS), :] * scaled_weight).astype(BF16)
            for i in range(2)
        ]
        sums = dot(hot, jnp.concatenate(pair, axis=1))
        for t in range(SUB):
            rows = slice(t * LEAVES, (t + 1) * LEAVES)
            tile = jnp.concatenate([sums[rows, :NODES], sums[rows, NODES:]], axis=0)
            send1[t, r * LEAVES:(r + 2) * LEAVES, :] = tile.astype(BF16)

    pl.semaphore_wait(barrier, len(peers))
    copies1 = start_all([
        remote(send1.at[t], recv1.at[d], s1.at[d], r1.at[d], (w, t)) for d, t in enumerate(subs)
    ])

    loads["edge0"].wait()
    loads["edge1"].wait()
    edge_send[0] = dot(basis[last, 0:RHS, :].astype(BF16), edge_corr[0])
    edge_send[1] = dot(basis[last, ROWS - RHS:, :].astype(BF16), edge_corr[1])
    edges = start_all([
        remote(edge_send.at[0], edge_recv.at[0], edge_s.at[0], edge_r.at[0], below_id),
        remote(edge_send.at[1], edge_recv.at[1], edge_s.at[1], edge_r.at[1], above_id),
    ])

    loads["multi"].wait()
    loads["up"].wait()

    def compose_up(leaf, carry):
        high, low = split(up[leaf])
        product = dot(multi[...], high) + dot(multi[...], low)
        rows = pl.ds(pl.multiple_of(leaf * NODES, NODES), NODES)
        up_high[rows, :], up_low[rows, :] = split(product)
        return carry

    lax.fori_loop(0, LEAVES, compose_up, 0)

    def near_one(p):
        def x(q):
            return basis[last, patch_rows(q), :].astype(BF16)

        return (
            dot(x(p), corr[3 * p + 1])
            + dot(x(p + 1), corr[3 * p + 3])
            + dot(x(p - 1), corr[3 * p - 1])
        )

    def near_range(first, end):
        def body(p, carry):
            image[patch_rows(p), :] = near_one(p)
            return carry

        lax.fori_loop(first, end, body, 0)

    chunk = PATCHES // NEAR_CHUNKS

    def near_chunk(c):
        corr_loads[c].wait()
        near_range(max(1, c * chunk - 1), (c + 1) * chunk - 1)

    near_chunk(0)

    for copy in copies1:
        copy.wait_recv()
    total = send1[s].astype(F32)
    for d in range(SUB - 1):
        total = total + recv1[d].astype(F32)
    sums1[...] = total
    lanes = jnp.concatenate(
        [sums1[pl.ds(leaf, RHS, stride=LEAVES), :] for leaf in range(LEAVES)], axis=1
    )
    tree = split_dot(lanes, up_high, up_low)
    send2[0] = tree[:, :NODES]
    send2[1] = tree[:, NODES:]
    copies2 = start_all([
        remote(send2.at[t // 4], recv2.at[d], s2.at[d], r2.at[d], (w, t)) for d, t in enumerate(subs)
    ])

    loads["far"].wait()
    far_high[...], far_low[...] = split(far[...])
    near_chunk(1)
    for copy in copies1:
        copy.wait_send()

    for copy in copies2:
        copy.wait_recv()
    half = send2[s // 4]
    for d in range(SUB - 1):
        half = half + recv2[d]
    lane = lax.broadcasted_iota(jnp.int32, (RHS, NODES), 1)
    mine = jnp.where(lane // SHARE == lax.rem(s, 4), half, 0.0)
    turn = lax.rem(lax.rem(w, 4) + 4 - lax.rem(s, 4), 4)
    placed = mine
    for k in range(1, 4):
        placed = jnp.where(turn == k, pltpu.roll(mine, k * SHARE, 1), placed)
    send3[...] = placed
    copies3 = start_all([
        remote(send3, recv3.at[w], s3.at[d], r3.at[w], (v, s)) for d, v in enumerate(wides)
    ])
    recv3[w] = placed

    loads["eval"].wait()
    loads["down"].wait()

    def compose_down(leaf, carry):
        high, low = split(down[leaf])
        product = dot(high, evalm[...]) + dot(low, evalm[...])
        columns = pl.ds(pl.multiple_of(leaf * NODES, NODES), NODES)
        down_high[:, columns], down_low[:, columns] = split(product)
        return carry

    lax.fori_loop(0, LEAVES, compose_down, 0)
    near_chunk(2)
    for copy in copies2:
        copy.wait_send()

    for d, v in enumerate(wide_sources):
        remote(send3, recv3.at[v], s3.at[d], r3.at[v], (v, s)).wait_recv()
    lanes = jnp.concatenate(
        [
            (recv3[4 * g] + recv3[4 * g + 1]) + (recv3[4 * g + 2] + recv3[4 * g + 3])
            for g in range(WIDE // 4)
        ],
        axis=1,
    )
    send4[...] = split_dot(lanes, far_high, far_low)
    copies4 = start_all([
        remote(send4, recv4.at[d], s4.at[d], r4.at[d], (w, t)) for d, t in enumerate(subs)
    ])

    for j in range(last):
        loads["basis%d" % j].wait()
    zero = jnp.zeros((RHS, NODES), F32)

    def gram_body(p, sums):
        rows = patch_rows(p)
        node_weight = jnp.broadcast_to(weight[pl.ds(p, 1), :], (RHS, NODES))
        vectors = [basis[j, rows, :] for j in range(BASIS)]
        weighted = [v * node_weight for v in vectors]
        return tuple(a + weighted[j] * vectors[k] for a, (j, k) in zip(sums, PAIRS))

    gram = lax.fori_loop(0, PATCHES, gram_body, (zero,) * len(PAIRS))
    packed = zero
    for i, value in enumerate(gram):
        packed = jnp.where(lane == BASIS + 1 + i, jnp.sum(value, axis=1, keepdims=True), packed)
    for copy in copies3:
        copy.wait_send()

    for copy in copies4:
        copy.wait_recv()
    local = send4[...]
    for d in range(SUB - 1):
        local = local + recv4[d]
    potentials = split_dot(local, down_high, down_low).astype(BF16)
    for leaf in range(LEAVES):
        field[s * LEAVES + leaf] = potentials[:, leaf * NODES:(leaf + 1) * NODES]
    own = pl.ds(s * LEAVES, LEAVES)
    copies5 = start_all([
        remote(field.at[own], field.at[own], s5.at[d], r5.at[s], (w, t)) for d, t in enumerate(subs)
    ])

    near_chunk(3)
    for copy in edges:
        copy.wait()

    def current_half(p):
        return basis[last, p * RHS:(p + 1) * RHS, :].astype(BF16)

    from_below = jnp.where(me > 0, edge_recv[1], 0.0)
    from_above = jnp.where(me < WIDE * SUB - 1, edge_recv[0], 0.0)
    end = PATCHES - 1
    image[0:RHS, :] = (
        dot(current_half(0), corr[1]) + dot(current_half(1), corr[3]) + from_below
    )
    image[end * RHS:, :] = (
        dot(current_half(end), corr[3 * end + 1])
        + dot(current_half(end - 1), corr[3 * end - 1])
        + from_above
    )
    for name in ("route_s", "slot_s"):
        loads[name].wait()
    for copy in copies4:
        copy.wait_send()

    for d in range(1, SUB):
        t = lax.rem(s + SUB - d, SUB)
        block = field.at[pl.ds(t * LEAVES, LEAVES)]
        remote(block, block, s5.at[d - 1], r5.at[t], (w, t)).wait_recv()

    def products_body(p, sums):
        rows = patch_rows(p)
        leaf = route_s[0, p] * LEAVES + slot_s[0, p]
        value = image[rows, :] + field[leaf].astype(F32)
        image[rows, :] = value
        weighted = value * jnp.broadcast_to(weight[pl.ds(p, 1), :], (RHS, NODES))
        return tuple(
            a + weighted * (basis[i, rows, :] if i < BASIS else value) for i, a in enumerate(sums)
        )

    products = lax.fori_loop(0, PATCHES, products_body, (zero,) * (BASIS + 1))
    for i, value in enumerate(products):
        packed = jnp.where(lane == i, jnp.sum(value, axis=1, keepdims=True), packed)
    low_rows = RHS // 2
    send6[...] = packed[:low_rows] + pltpu.roll(packed[low_rows:], RHS, 1)
    copies6 = start_all([
        remote(send6, recv6.at[s], s6.at[d], r6.at[s], (w, t)) for d, t in enumerate(subs)
    ])
    recv6[s] = send6[...]
    for copy in copies5:
        copy.wait_send()
    for d in range(1, SUB):
        t = lax.rem(s + SUB - d, SUB)
        remote(send6, recv6.at[t], s6.at[d - 1], r6.at[t], (w, t)).wait_recv()
    total6 = recv6[0]
    for t in range(1, SUB):
        total6 = total6 + recv6[t]
    send7[...] = total6
    copies7 = start_all([
        remote(send7, recv7.at[w], s7.at[d], r7.at[w], (v, s)) for d, v in enumerate(wides)
    ])
    recv7[w] = total6
    for copy in copies6:
        copy.wait_send()
    for d, v in enumerate(wide_sources):
        remote(send7, recv7.at[v], s7.at[d], r7.at[v], (v, s)).wait_recv()
    total7 = recv7[0]
    for v in range(1, WIDE):
        total7 = total7 + recv7[v]
    total7 = total7 * (1.0 / TOTAL)
    full = jnp.concatenate([total7, pltpu.roll(total7, NODES - RHS, 1)], axis=0)

    def column(i):
        return full[:, i:i + 1]

    gram_of = {}
    for i, (j, k) in enumerate(PAIRS):
        gram_of[j, k] = gram_of[k, j] = column(BASIS + 1 + i)
    fields = [column(j) for j in range(BASIS)]
    first = [fields[j] + 0.5 * gram_of[j, last] for j in range(BASIS)]
    coeffs = []
    for j in range(BASIS):
        second = first[j]
        for k in range(BASIS):
            second = second - gram_of[j, k] * first[k]
        coeffs.append(first[j] + second)
    deltas = [coeffs[j] - 0.5 if j == last else coeffs[j] for j in range(BASIS)]
    square = column(BASIS)
    for j in range(BASIS):
        inner = -2.0 * fields[j]
        for k in range(BASIS):
            inner = inner + gram_of[j, k] * deltas[k]
        square = square + deltas[j] * inner
    beta = jnp.sqrt(jnp.maximum(square, 0.0) + 1e-6)
    inverse = jnp.broadcast_to(1.0 / beta, (RHS, NODES))
    factors = [jnp.broadcast_to(value, (RHS, NODES)) * inverse for value in deltas]

    def final_body(p, carry):
        rows = patch_rows(p)
        value = image[rows, :] * inverse
        for j in range(BASIS):
            value = value - factors[j] * basis[j, rows, :]
        vector_out[rows, :] = value
        return carry

    lax.fori_loop(0, PATCHES, final_body, 0)
    row = lax.broadcasted_iota(jnp.int32, (RHS, NODES), 0)
    columns = coeffs + [beta]
    for i, value in enumerate(columns):
        flat = jnp.sum(jnp.where(row == lane, value, 0.0), axis=0, keepdims=True)
        hess_out[i:i + 1, :] = flat[:, :RHS]
    for copy in copies7:
        copy.wait_send()


def per_device(
    krylov_basis, quad_weight, corrections, patch_route, leaf_slot, multipole_map,
    upward_translation, far_coupling, downward_translation, evaluation_map,
):
    anywhere = pl.BlockSpec(memory_space=pl.ANY)
    inside = pl.BlockSpec(memory_space=pltpu.VMEM)
    dma = pltpu.SemaphoreType.DMA
    near_blocks = 3 * PATCHES
    vector, hessenberg = pl.pallas_call(
        kernel,
        out_shape=(
            jax.ShapeDtypeStruct((ROWS, NODES), F32),
            jax.ShapeDtypeStruct((BASIS + 1, RHS), F32),
        ),
        in_specs=[anywhere] * 10,
        out_specs=(inside, inside),
        scratch_shapes=[
            pltpu.VMEM((BASIS, ROWS, NODES), F32),
            pltpu.VMEM((PATCHES, NODES), F32),
            pltpu.VMEM((near_blocks, NODES, NODES), BF16),
            pltpu.VMEM((1, PATCHES), jnp.int32),
            pltpu.VMEM((1, PATCHES), jnp.int32),
            pltpu.SMEM((1, PATCHES), jnp.int32),
            pltpu.SMEM((1, PATCHES), jnp.int32),
            pltpu.VMEM((NODES, COEFFS), BF16),
            pltpu.VMEM((LEAVES, COEFFS, COEFFS), F32),
            pltpu.VMEM((WIDE * SHARE, COEFFS), F32),
            pltpu.VMEM((LEAVES, COEFFS, COEFFS), F32),
            pltpu.VMEM((COEFFS, NODES), BF16),
            pltpu.VMEM((2, NODES, NODES), BF16),
            pltpu.VMEM((LEAVES * NODES, COEFFS), BF16),
            pltpu.VMEM((LEAVES * NODES, COEFFS), BF16),
            pltpu.VMEM((WIDE * SHARE, COEFFS), BF16),
            pltpu.VMEM((WIDE * SHARE, COEFFS), BF16),
            pltpu.VMEM((COEFFS, LEAVES * NODES), BF16),
            pltpu.VMEM((COEFFS, LEAVES * NODES), BF16),
            pltpu.VMEM((ROWS, NODES), F32),
            pltpu.VMEM((SUB, RHS * LEAVES, NODES), BF16),
            pltpu.VMEM((SUB - 1, RHS * LEAVES, NODES), BF16),
            pltpu.VMEM((RHS * LEAVES, NODES), F32),
            pltpu.VMEM((2, RHS, NODES), F32),
            pltpu.VMEM((SUB - 1, RHS, NODES), F32),
            pltpu.VMEM((RHS, NODES), F32),
            pltpu.VMEM((WIDE, RHS, NODES), F32),
            pltpu.VMEM((RHS, COEFFS), F32),
            pltpu.VMEM((SUB - 1, RHS, COEFFS), F32),
            pltpu.VMEM((SUB * LEAVES, RHS, NODES), BF16),
            pltpu.VMEM((2, RHS, NODES), F32),
            pltpu.VMEM((2, RHS, NODES), F32),
            pltpu.VMEM((RHS // 2, NODES), F32),
            pltpu.VMEM((SUB, RHS // 2, NODES), F32),
            pltpu.VMEM((RHS // 2, NODES), F32),
            pltpu.VMEM((WIDE, RHS // 2, NODES), F32),
            dma((16,)), dma((NEAR_CHUNKS,)), dma((2,)), dma((2,)),
            dma((SUB - 1,)), dma((SUB - 1,)),
            dma((SUB - 1,)), dma((SUB - 1,)),
            dma((WIDE - 1,)), dma((WIDE,)),
            dma((SUB - 1,)), dma((SUB - 1,)),
            dma((SUB - 1,)), dma((SUB,)),
            dma((SUB - 1,)), dma((SUB,)),
            dma((WIDE - 1,)), dma((WIDE,)),
        ],
        compiler_params=pltpu.CompilerParams(
            collective_id=0, has_side_effects=True, vmem_limit_bytes=40 << 20
        ),
    )(
        krylov_basis.reshape(BASIS, ROWS, NODES),
        quad_weight,
        corrections.reshape(near_blocks, NODES, NODES),
        patch_route.reshape(1, PATCHES),
        leaf_slot.reshape(1, PATCHES),
        multipole_map,
        upward_translation,
        far_coupling.reshape(WIDE * SHARE, COEFFS),
        downward_translation,
        evaluation_map,
    )
    return vector.reshape(PATCHES, RHS, NODES), hessenberg


def solution(mesh):
    return jax.shard_map(
        per_device,
        mesh=mesh,
        in_specs=(
            P(None, ("wide", "sub"), None, None),
            P(("wide", "sub"), None),
            P(("wide", "sub"), None, None, None),
            P(("wide", "sub"), None),
            P(("wide", "sub")),
            P(),
            P(("wide", "sub"), None, None),
            P("wide", None, "sub", None),
            P(("wide", "sub"), None, None),
            P(),
        ),
        out_specs=(P(("wide", "sub"), None, None), P()),
        check_vma=False,
    )
```

```python
import functools

import jax
import jax.numpy as jnp
from jax import lax
from jax.experimental import pallas as pl
from jax.experimental.pallas import tpu as pltpu
from jax.sharding import PartitionSpec as P

MESH = pl.DeviceIdType.MESH
F32 = jnp.float32
BF16 = jnp.bfloat16
WIDE, SUB = 16, 8
PATCHES, RHS, NODES, COEFFS, BASIS, LEAVES = 128, 16, 128, 256, 4, 8
SHARE = COEFFS // SUB
ROWS = PATCHES * RHS
TOTAL = float(WIDE * SUB * PATCHES * NODES)
SCALE = 1.0 / 32.0
PAIRS = [(j, k) for j in range(BASIS) for k in range(j, BASIS)]
NEAR_CHUNKS = 4


def split(value):
    high = value.astype(BF16)
    return high, (value - high.astype(F32)).astype(BF16)


def dot(a, b):
    return jnp.dot(a, b, preferred_element_type=F32)


def split_dot(value, high_ref, low_ref):
    high, low = split(value)
    rows = value.shape[0]
    both = dot(jnp.concatenate([high, low], axis=0), high_ref[...])
    return both[:rows] + both[rows:] + dot(high, low_ref[...])


def patch_rows(p):
    return pl.ds(pl.multiple_of(p * RHS, RHS), RHS)


def kernel(
    basis_hbm, weight_hbm, corr_hbm, route_hbm, slot_hbm, multi_hbm, up_hbm, far_hbm, down_hbm,
    eval_hbm, vector_out, hess_out,
    basis, weight, corr, route_v, slot_v, route_s, slot_s, multi, up, far, down, evalm, edge_corr,
    up_high, up_low, far_high, far_low, down_high, down_low, image,
    send1, recv1, sums1, send2, recv2, send3, recv3, send4, recv4, field,
    edge_send, edge_recv, send6, recv6, send7, recv7, bulk_send, bulk_recv, bulk_sums, area_send, area_recv,
    load_sem, corr_sem, edge_s, edge_r, s1, r1, s2, r2, s3, r3, s4, r4, s5, r5, s6, r6, s7, r7,
    s8, r8, s9, r9, s10, r10,
):
    w = lax.axis_index("wide")
    s = lax.axis_index("sub")
    me = w * SUB + s
    below = lax.rem(me + WIDE * SUB - 1, WIDE * SUB)
    above = lax.rem(me + 1, WIDE * SUB)
    below_id = (below // SUB, lax.rem(below, SUB))
    above_id = (above // SUB, lax.rem(above, SUB))
    subs = [lax.rem(s + d, SUB) for d in range(1, SUB)]
    wides = [lax.rem(w + d, WIDE) for d in range(1, WIDE)]
    wide_sources = [lax.rem(w + WIDE - d, WIDE) for d in range(1, WIDE)]

    barrier = pltpu.get_barrier_semaphore()
    peers = [(w, t) for t in subs] + [(v, s) for v in wides] + [below_id, above_id]
    for peer in peers:
        pl.semaphore_signal(barrier, inc=1, device_id=peer, device_id_type=MESH)

    last = BASIS - 1
    loads = {}

    def load(name, source, target):
        copy = pltpu.make_async_copy(source, target, load_sem.at[len(loads)])
        copy.start()
        loads[name] = copy

    load("current", basis_hbm.at[last], basis.at[last])
    load("weight", weight_hbm, weight)
    load("route_v", route_hbm, route_v)
    load("slot_v", slot_hbm, slot_v)
    load("multi", multi_hbm, multi)
    load("up", up_hbm, up)
    load("edge0", corr_hbm.at[0], edge_corr.at[0])
    load("edge1", corr_hbm.at[3 * PATCHES - 1], edge_corr.at[1])
    load("basis", basis_hbm.at[pl.ds(0, last)], basis.at[pl.ds(0, last)])
    load("route_s", route_hbm, route_s)
    load("slot_s", slot_hbm, slot_s)
    blocks = 3 * PATCHES // NEAR_CHUNKS
    corr_loads = []
    for c in range(NEAR_CHUNKS):
        copy = pltpu.make_async_copy(
            corr_hbm.at[pl.ds(c * blocks, blocks)], corr.at[pl.ds(c * blocks, blocks)], corr_sem.at[c]
        )
        copy.start()
        corr_loads.append(copy)
    load("far", far_hbm, far)
    load("eval", eval_hbm, evalm)
    load("down", down_hbm, down)

    def start_all(copies):
        for copy in copies:
            copy.start()
        return copies

    def remote(source, target, send_sem, recv_sem, device):
        return pltpu.make_async_remote_copy(
            src_ref=source, dst_ref=target, send_sem=send_sem, recv_sem=recv_sem,
            device_id=device, device_id_type=MESH,
        )

    for name in ("current", "weight", "route_v", "slot_v"):
        loads[name].wait()
    leaf_row = route_v[...] * LEAVES + slot_v[...]
    leaf_count = SUB * LEAVES
    hot = (
        lax.broadcasted_iota(jnp.int32, (leaf_count, PATCHES), 0)
        == jnp.broadcast_to(leaf_row, (leaf_count, PATCHES))
    ).astype(F32).astype(BF16)
    scaled_weight = weight[...] * SCALE

    def leaf_sums(read, store):
        for r in range(0, RHS, 2):
            pair = [(read(pl.ds(r + i, PATCHES, stride=RHS)) * scaled_weight).astype(BF16) for i in range(2)]
            sums = dot(hot, jnp.concatenate(pair, axis=1))
            for t in range(SUB):
                rows = slice(t * LEAVES, (t + 1) * LEAVES)
                tile = jnp.concatenate([sums[rows, :NODES], sums[rows, NODES:]], axis=0)
                store(t, slice(r * LEAVES, (r + 2) * LEAVES), tile.astype(BF16))

    def store1(t, rows, tile):
        send1[t, rows, :] = tile

    leaf_sums(lambda rows: basis[last, rows, :], store1)

    pl.semaphore_wait(barrier, len(peers))
    copies1 = start_all([
        remote(send1.at[t], recv1.at[d], s1.at[d], r1.at[d], (w, t)) for d, t in enumerate(subs)
    ])

    loads["edge0"].wait()
    loads["edge1"].wait()
    edge_send[0] = dot(basis[last, 0:RHS, :].astype(BF16), edge_corr[0])
    edge_send[1] = dot(basis[last, ROWS - RHS:, :].astype(BF16), edge_corr[1])
    edges = start_all([
        remote(edge_send.at[0], edge_recv.at[0], edge_s.at[0], edge_r.at[0], below_id),
        remote(edge_send.at[1], edge_recv.at[1], edge_s.at[1], edge_r.at[1], above_id),
    ])

    loads["multi"].wait()
    loads["up"].wait()

    def compose_up(leaf, carry):
        high, low = split(up[leaf])
        product = dot(multi[...], high) + dot(multi[...], low)
        rows = pl.ds(pl.multiple_of(leaf * NODES, NODES), NODES)
        up_high[rows, :], up_low[rows, :] = split(product)
        return carry

    lax.fori_loop(0, LEAVES, compose_up, 0)

    def half(p):
        return basis[last, patch_rows(p), :].astype(BF16)

    def near_pair(h, carry):
        p = 2 * h + 1
        left = jnp.concatenate([half(p), half(p + 1)], axis=1)
        right = jnp.concatenate(
            [
                jnp.concatenate([corr[3 * p + 1], corr[3 * p + 2]], axis=1),
                jnp.concatenate([corr[3 * p + 3], corr[3 * p + 4]], axis=1),
            ],
            axis=0,
        )
        both = dot(left, right)
        image[patch_rows(p), :] = both[:, :NODES] + dot(half(p - 1), corr[3 * p - 1])
        image[patch_rows(p + 1), :] = both[:, NODES:] + dot(half(p + 2), corr[3 * p + 6])
        return carry

    chunk = PATCHES // NEAR_CHUNKS // 2

    def near_chunk(c):
        corr_loads[c].wait()
        lax.fori_loop(max(0, c * chunk - 1), (c + 1) * chunk - 1, near_pair, 0, unroll=5 if c == 0 else 8)

    def bulk_store(j):
        def store(t, rows, tile):
            bulk_send[t, j, rows, :] = tile

        return store

    loads["basis"].wait()
    for j in range(last):
        leaf_sums(functools.partial(lambda k, rows: basis[k, rows, :], j), bulk_store(j))
    area_high, area_low = split(weight[...])
    areas = dot(hot, area_high) + dot(hot, area_low)
    for t in range(SUB):
        area_send[t] = areas[t * LEAVES:(t + 1) * LEAVES]
    near_chunk(0)
    near_chunk(1)

    for copy in copies1:
        copy.wait_recv()
    total = send1[s].astype(F32)
    for d in range(SUB - 1):
        total = total + recv1[d].astype(F32)
    sums1[...] = total
    lanes = jnp.concatenate(
        [sums1[pl.ds(leaf, RHS, stride=LEAVES), :] for leaf in range(LEAVES)], axis=1
    )
    tree = split_dot(lanes, up_high, up_low)
    send2[0] = tree[:, :NODES]
    send2[1] = tree[:, NODES:]
    copies2 = start_all([
        remote(send2.at[t // 4], recv2.at[d], s2.at[d], r2.at[d], (w, t)) for d, t in enumerate(subs)
    ])

    copies8 = start_all([
        remote(bulk_send.at[t, pl.ds(0, last)], bulk_recv.at[d, pl.ds(0, last)], s8.at[d], r8.at[d], (w, t))
        for d, t in enumerate(subs)
    ] + [
        remote(area_send.at[t], area_recv.at[d], s9.at[d], r9.at[d], (w, t)) for d, t in enumerate(subs)
    ])

    loads["far"].wait()
    far_high[...], far_low[...] = split(far[...])
    near_chunk(2)
    near_chunk(3)
    for copy in edges:
        copy.wait()

    def current_half(p):
        return basis[last, p * RHS:(p + 1) * RHS, :].astype(BF16)

    from_below = jnp.where(me > 0, edge_recv[1], 0.0)
    from_above = jnp.where(me < WIDE * SUB - 1, edge_recv[0], 0.0)
    end = PATCHES - 1
    image[0:RHS, :] = (
        dot(current_half(0), corr[1]) + dot(current_half(1), corr[3]) + from_below
    )
    image[end * RHS:, :] = (
        dot(current_half(end), corr[3 * end + 1])
        + dot(current_half(end - 1), corr[3 * end - 1])
        + from_above
    )
    for copy in copies1:
        copy.wait_send()

    for copy in copies2:
        copy.wait_recv()
    half_tree = send2[s // 4]
    for d in range(SUB - 1):
        half_tree = half_tree + recv2[d]
    lane = lax.broadcasted_iota(jnp.int32, (RHS, NODES), 1)
    mine = jnp.where(lane // SHARE == lax.rem(s, 4), half_tree, 0.0)
    turn = lax.rem(lax.rem(w, 4) + 4 - lax.rem(s, 4), 4)
    placed = mine
    for k in range(1, 4):
        placed = jnp.where(turn == k, pltpu.roll(mine, k * SHARE, 1), placed)
    send3[...] = placed
    copies3 = start_all([
        remote(send3, recv3.at[w], s3.at[d], r3.at[w], (v, s)) for d, v in enumerate(wides)
    ])
    recv3[w] = placed

    leaf_sums(lambda rows: image[rows, :], bulk_store(last))
    copies10 = start_all([
        remote(bulk_send.at[t, last], bulk_recv.at[d, last], s10.at[d], r10.at[d], (w, t))
        for d, t in enumerate(subs)
    ])

    loads["eval"].wait()
    loads["down"].wait()

    def compose_down(leaf, carry):
        high, low = split(down[leaf])
        product = dot(high, evalm[...]) + dot(low, evalm[...])
        columns = pl.ds(pl.multiple_of(leaf * NODES, NODES), NODES)
        down_high[:, columns], down_low[:, columns] = split(product)
        return carry

    lax.fori_loop(0, LEAVES, compose_down, 0)
    zero = jnp.zeros((RHS, NODES), F32)

    def node_weight(p):
        return jnp.broadcast_to(weight[pl.ds(p, 1), :], (RHS, NODES))

    def gram_body(p, sums):
        rows = patch_rows(p)
        vectors = [basis[j, rows, :] for j in range(BASIS)]
        weighted = [v * node_weight(p) for v in vectors]
        return tuple(a + weighted[j] * vectors[k] for a, (j, k) in zip(sums, PAIRS))

    gram = lax.fori_loop(0, PATCHES, gram_body, (zero,) * len(PAIRS), unroll=2)
    packed = zero
    for i, value in enumerate(gram):
        packed = jnp.where(lane == BASIS + 1 + i, jnp.sum(value, axis=1, keepdims=True), packed)
    for copy in copies2:
        copy.wait_send()

    for d, v in enumerate(wide_sources):
        remote(send3, recv3.at[v], s3.at[d], r3.at[v], (v, s)).wait_recv()
    lanes = jnp.concatenate(
        [
            (recv3[4 * g] + recv3[4 * g + 1]) + (recv3[4 * g + 2] + recv3[4 * g + 3])
            for g in range(WIDE // 4)
        ],
        axis=1,
    )
    send4[...] = split_dot(lanes, far_high, far_low)
    copies4 = start_all([
        remote(send4, recv4.at[d], s4.at[d], r4.at[d], (w, t)) for d, t in enumerate(subs)
    ])

    def near_products(p, sums):
        rows = patch_rows(p)
        value = image[rows, :]
        weighted = value * node_weight(p)
        return tuple(
            a + weighted * (basis[i, rows, :] if i < BASIS else value) for i, a in enumerate(sums)
        )

    products = lax.fori_loop(0, PATCHES, near_products, (zero,) * (BASIS + 1), unroll=2)
    for copy in copies3:
        copy.wait_send()
    for copy in copies8 + copies10:
        copy.wait_recv()
    for j in range(BASIS):
        total = bulk_send[s, j].astype(F32)
        for d in range(SUB - 1):
            total = total + bulk_recv[d, j].astype(F32)
        bulk_sums[j] = total
    area = area_send[s]
    for d in range(SUB - 1):
        area = area + area_recv[d]

    for copy in copies4:
        copy.wait_recv()
    local = send4[...]
    for d in range(SUB - 1):
        local = local + recv4[d]
    potentials = split_dot(local, down_high, down_low).astype(BF16)
    far_sums = [zero] * (BASIS + 2)
    for leaf in range(LEAVES):
        field[s * LEAVES + leaf] = potentials[:, leaf * NODES:(leaf + 1) * NODES]
        value = potentials[:, leaf * NODES:(leaf + 1) * NODES].astype(F32)
        rows = pl.ds(leaf, RHS, stride=LEAVES)
        others = [bulk_sums[j, rows, :] for j in range(last)]
        others += [sums1[rows, :], bulk_sums[last, rows, :]]
        others += [value * jnp.broadcast_to(area[leaf:leaf + 1], (RHS, NODES))]
        far_sums = [a + value * b for a, b in zip(far_sums, others)]
    products = [products[j] + far_sums[j] * (1.0 / SCALE) for j in range(BASIS)] + [
        products[BASIS] + far_sums[BASIS] * (2.0 / SCALE) + far_sums[BASIS + 1]
    ]
    for i, value in enumerate(products):
        packed = jnp.where(lane == i, jnp.sum(value, axis=1, keepdims=True), packed)
    low_rows = RHS // 2
    share = packed[:low_rows] + pltpu.roll(packed[low_rows:], RHS, 1)
    send7[...] = share
    copies7 = start_all([
        remote(send7, recv7.at[w], s7.at[d], r7.at[w], (v, s)) for d, v in enumerate(wides)
    ])
    recv7[w] = share
    own = pl.ds(s * LEAVES, LEAVES)
    copies5 = start_all([
        remote(field.at[own], field.at[own], s5.at[d], r5.at[s], (w, t)) for d, t in enumerate(subs)
    ])
    for name in ("route_s", "slot_s"):
        loads[name].wait()
    for copy in copies4 + copies8 + copies10:
        copy.wait_send()

    for d, v in enumerate(wide_sources):
        remote(send7, recv7.at[v], s7.at[d], r7.at[v], (v, s)).wait_recv()
    total7 = recv7[0]
    for v in range(1, WIDE):
        total7 = total7 + recv7[v]
    send6[...] = total7
    copies6 = start_all([
        remote(send6, recv6.at[s], s6.at[d], r6.at[s], (w, t)) for d, t in enumerate(subs)
    ])
    recv6[s] = total7

    for d in range(1, SUB):
        t = lax.rem(s + SUB - d, SUB)
        block = field.at[pl.ds(t * LEAVES, LEAVES)]
        remote(block, block, s5.at[d - 1], r5.at[t], (w, t)).wait_recv()

    def add_far(p, carry):
        rows = patch_rows(p)
        leaf = route_s[0, p] * LEAVES + slot_s[0, p]
        image[rows, :] = image[rows, :] + field[leaf].astype(F32)
        return carry

    lax.fori_loop(0, PATCHES, add_far, 0, unroll=4)
    for copy in copies5 + copies7:
        copy.wait_send()
    for d in range(1, SUB):
        t = lax.rem(s + SUB - d, SUB)
        remote(send6, recv6.at[t], s6.at[d - 1], r6.at[t], (w, t)).wait_recv()
    total7 = recv6[0]
    for t in range(1, SUB):
        total7 = total7 + recv6[t]
    total7 = total7 * (1.0 / TOTAL)
    full = jnp.concatenate([total7, pltpu.roll(total7, NODES - RHS, 1)], axis=0)

    def column(i):
        return full[:, i:i + 1]

    gram_of = {}
    for i, (j, k) in enumerate(PAIRS):
        gram_of[j, k] = gram_of[k, j] = column(BASIS + 1 + i)
    fields = [column(j) for j in range(BASIS)]
    first = [fields[j] + 0.5 * gram_of[j, last] for j in range(BASIS)]
    coeffs = []
    for j in range(BASIS):
        second = first[j]
        for k in range(BASIS):
            second = second - gram_of[j, k] * first[k]
        coeffs.append(first[j] + second)
    deltas = [coeffs[j] - 0.5 if j == last else coeffs[j] for j in range(BASIS)]
    square = column(BASIS)
    for j in range(BASIS):
        inner = -2.0 * fields[j]
        for k in range(BASIS):
            inner = inner + gram_of[j, k] * deltas[k]
        square = square + deltas[j] * inner
    beta = jnp.sqrt(jnp.maximum(square, 0.0) + 1e-6)
    inverse = jnp.broadcast_to(1.0 / beta, (RHS, NODES))
    factors = [jnp.broadcast_to(value, (RHS, NODES)) * inverse for value in deltas]

    def final_body(p, carry):
        rows = patch_rows(p)
        value = image[rows, :] * inverse
        for j in range(BASIS):
            value = value - factors[j] * basis[j, rows, :]
        vector_out[rows, :] = value
        return carry

    lax.fori_loop(0, PATCHES, final_body, 0, unroll=4)
    row = lax.broadcasted_iota(jnp.int32, (RHS, NODES), 0)
    columns = coeffs + [beta]
    for i, value in enumerate(columns):
        flat = jnp.sum(jnp.where(row == lane, value, 0.0), axis=0, keepdims=True)
        hess_out[i:i + 1, :] = flat[:, :RHS]
    for copy in copies6:
        copy.wait_send()


def per_device(
    krylov_basis, quad_weight, corrections, patch_route, leaf_slot, multipole_map,
    upward_translation, far_coupling, downward_translation, evaluation_map,
):
    outside = pl.BlockSpec(memory_space=pl.ANY)
    inside = pl.BlockSpec(memory_space=pltpu.VMEM)
    dma = pltpu.SemaphoreType.DMA
    near_blocks = 3 * PATCHES
    vector, hessenberg = pl.pallas_call(
        kernel,
        out_shape=(
            jax.ShapeDtypeStruct((ROWS, NODES), F32),
            jax.ShapeDtypeStruct((BASIS + 1, RHS), F32),
        ),
        in_specs=[outside] * 10,
        out_specs=(inside, inside),
        scratch_shapes=[
            pltpu.VMEM((BASIS, ROWS, NODES), F32),
            pltpu.VMEM((PATCHES, NODES), F32),
            pltpu.VMEM((near_blocks, NODES, NODES), BF16),
            pltpu.VMEM((1, PATCHES), jnp.int32),
            pltpu.VMEM((1, PATCHES), jnp.int32),
            pltpu.SMEM((1, PATCHES), jnp.int32),
            pltpu.SMEM((1, PATCHES), jnp.int32),
            pltpu.VMEM((NODES, COEFFS), BF16),
            pltpu.VMEM((LEAVES, COEFFS, COEFFS), F32),
            pltpu.VMEM((WIDE * SHARE, COEFFS), F32),
            pltpu.VMEM((LEAVES, COEFFS, COEFFS), F32),
            pltpu.VMEM((COEFFS, NODES), BF16),
            pltpu.VMEM((2, NODES, NODES), BF16),
            pltpu.VMEM((LEAVES * NODES, COEFFS), BF16),
            pltpu.VMEM((LEAVES * NODES, COEFFS), BF16),
            pltpu.VMEM((WIDE * SHARE, COEFFS), BF16),
            pltpu.VMEM((WIDE * SHARE, COEFFS), BF16),
            pltpu.VMEM((COEFFS, LEAVES * NODES), BF16),
            pltpu.VMEM((COEFFS, LEAVES * NODES), BF16),
            pltpu.VMEM((ROWS, NODES), F32),
            pltpu.VMEM((SUB, RHS * LEAVES, NODES), BF16),
            pltpu.VMEM((SUB - 1, RHS * LEAVES, NODES), BF16),
            pltpu.VMEM((RHS * LEAVES, NODES), F32),
            pltpu.VMEM((2, RHS, NODES), F32),
            pltpu.VMEM((SUB - 1, RHS, NODES), F32),
            pltpu.VMEM((RHS, NODES), F32),
            pltpu.VMEM((WIDE, RHS, NODES), F32),
            pltpu.VMEM((RHS, COEFFS), F32),
            pltpu.VMEM((SUB - 1, RHS, COEFFS), F32),
            pltpu.VMEM((SUB * LEAVES, RHS, NODES), BF16),
            pltpu.VMEM((2, RHS, NODES), F32),
            pltpu.VMEM((2, RHS, NODES), F32),
            pltpu.VMEM((RHS // 2, NODES), F32),
            pltpu.VMEM((SUB, RHS // 2, NODES), F32),
            pltpu.VMEM((RHS // 2, NODES), F32),
            pltpu.VMEM((WIDE, RHS // 2, NODES), F32),
            pltpu.VMEM((SUB, BASIS, RHS * LEAVES, NODES), BF16),
            pltpu.VMEM((SUB - 1, BASIS, RHS * LEAVES, NODES), BF16),
            pltpu.VMEM((BASIS, RHS * LEAVES, NODES), F32),
            pltpu.VMEM((SUB, LEAVES, NODES), F32),
            pltpu.VMEM((SUB - 1, LEAVES, NODES), F32),
            dma((16,)), dma((NEAR_CHUNKS,)), dma((2,)), dma((2,)),
            dma((SUB - 1,)), dma((SUB - 1,)),
            dma((SUB - 1,)), dma((SUB - 1,)),
            dma((WIDE - 1,)), dma((WIDE,)),
            dma((SUB - 1,)), dma((SUB - 1,)),
            dma((SUB - 1,)), dma((SUB,)),
            dma((SUB - 1,)), dma((SUB,)),
            dma((WIDE - 1,)), dma((WIDE,)),
            dma((SUB - 1,)), dma((SUB - 1,)),
            dma((SUB - 1,)), dma((SUB - 1,)),
            dma((SUB - 1,)), dma((SUB - 1,)),
        ],
        compiler_params=pltpu.CompilerParams(
            collective_id=0, has_side_effects=True, vmem_limit_bytes=60 << 20
        ),
    )(
        krylov_basis.reshape(BASIS, ROWS, NODES),
        quad_weight,
        corrections.reshape(near_blocks, NODES, NODES),
        patch_route.reshape(1, PATCHES),
        leaf_slot.reshape(1, PATCHES),
        multipole_map,
        upward_translation,
        far_coupling.reshape(WIDE * SHARE, COEFFS),
        downward_translation,
        evaluation_map,
    )
    return vector.reshape(PATCHES, RHS, NODES), hessenberg


def solution(mesh):
    return jax.shard_map(
        per_device,
        mesh=mesh,
        in_specs=(
            P(None, ("wide", "sub"), None, None),
            P(("wide", "sub"), None),
            P(("wide", "sub"), None, None, None),
            P(("wide", "sub"), None),
            P(("wide", "sub")),
            P(),
            P(("wide", "sub"), None, None),
            P("wide", None, "sub", None),
            P(("wide", "sub"), None, None),
            P(),
        ),
        out_specs=(P(("wide", "sub"), None, None), P()),
        check_vma=False,
    )
```

```python
import functools

import jax
import jax.numpy as jnp
from jax import lax
from jax.experimental import pallas as pl
from jax.experimental.pallas import tpu as pltpu
from jax.sharding import PartitionSpec as P

MESH = pl.DeviceIdType.MESH
F32 = jnp.float32
BF16 = jnp.bfloat16
WIDE, SUB = 16, 8
PATCHES, RHS, NODES, COEFFS, BASIS, LEAVES = 128, 16, 128, 256, 4, 8
SHARE = COEFFS // SUB
ROWS = PATCHES * RHS
TOTAL = float(WIDE * SUB * PATCHES * NODES)
SCALE = 1.0 / 32.0
PAIRS = [(j, k) for j in range(BASIS) for k in range(j, BASIS)]
NEAR_CHUNKS = 4


def split(value):
    high = value.astype(BF16)
    return high, (value - high.astype(F32)).astype(BF16)


def dot(a, b):
    return jnp.dot(a, b, preferred_element_type=F32)


def split_dot(value, high_ref, low_ref):
    high, low = split(value)
    rows = value.shape[0]
    both = dot(jnp.concatenate([high, low], axis=0), high_ref[...])
    return both[:rows] + both[rows:] + dot(high, low_ref[...])


def patch_rows(p):
    return pl.ds(pl.multiple_of(p * RHS, RHS), RHS)


def kernel(
    basis_hbm, weight_hbm, corr_hbm, route_hbm, slot_hbm, multi_hbm, up_hbm, far_hbm, down_hbm,
    eval_hbm, vector_out, hess_out,
    basis, weight, corr, route_v, slot_v, route_s, slot_s, multi, up, far, down, evalm, edge_corr,
    up_high, up_low, far_high, far_low, down_high, down_low, image,
    send1, recv1, sums1, send2, recv2, send3, recv3, send4, recv4, field,
    edge_send, edge_recv, send6, recv6, send7, recv7, bulk_send, pair_recv, pair_sums, bulk_recv, bulk_sums, area_send, area_recv,
    load_sem, corr_sem, edge_s, edge_r, s1, r1, s2, r2, s3, r3, s4, r4, s5, r5, s6, r6, s7, r7,
    s8, r8, s9, r9, s10, r10, pair_s, pair_r,
):
    w = lax.axis_index("wide")
    s = lax.axis_index("sub")
    me = w * SUB + s
    below = lax.rem(me + WIDE * SUB - 1, WIDE * SUB)
    above = lax.rem(me + 1, WIDE * SUB)
    below_id = (below // SUB, lax.rem(below, SUB))
    above_id = (above // SUB, lax.rem(above, SUB))
    subs = [lax.rem(s + d, SUB) for d in range(1, SUB)]
    core = lax.rem(s, 2)
    sibling = (w, s + 1 - 2 * core)
    columns_z = [(lax.rem(s // 2 + d, SUB // 2), d - 1) for d in range(1, SUB // 2)]
    wides = [lax.rem(w + d, WIDE) for d in range(1, WIDE)]
    wide_sources = [lax.rem(w + WIDE - d, WIDE) for d in range(1, WIDE)]

    barrier = pltpu.get_barrier_semaphore()
    peers = [(w, t) for t in subs] + [(v, s) for v in wides] + [below_id, above_id]
    for peer in peers:
        pl.semaphore_signal(barrier, inc=1, device_id=peer, device_id_type=MESH)

    last = BASIS - 1
    loads = {}

    def load(name, source, target):
        copy = pltpu.make_async_copy(source, target, load_sem.at[len(loads)])
        copy.start()
        loads[name] = copy

    load("current", basis_hbm.at[last], basis.at[last])
    load("weight", weight_hbm, weight)
    load("route_v", route_hbm, route_v)
    load("slot_v", slot_hbm, slot_v)
    load("multi", multi_hbm, multi)
    load("up", up_hbm, up)
    load("edge0", corr_hbm.at[0], edge_corr.at[0])
    load("edge1", corr_hbm.at[3 * PATCHES - 1], edge_corr.at[1])
    load("basis", basis_hbm.at[pl.ds(0, last)], basis.at[pl.ds(0, last)])
    load("route_s", route_hbm, route_s)
    load("slot_s", slot_hbm, slot_s)
    blocks = 3 * PATCHES // NEAR_CHUNKS
    corr_loads = []
    for c in range(NEAR_CHUNKS):
        copy = pltpu.make_async_copy(
            corr_hbm.at[pl.ds(c * blocks, blocks)], corr.at[pl.ds(c * blocks, blocks)], corr_sem.at[c]
        )
        copy.start()
        corr_loads.append(copy)
    load("far", far_hbm, far)
    load("eval", eval_hbm, evalm)
    load("down", down_hbm, down)

    def start_all(copies):
        for copy in copies:
            copy.start()
        return copies

    def remote(source, target, send_sem, recv_sem, device):
        return pltpu.make_async_remote_copy(
            src_ref=source, dst_ref=target, send_sem=send_sem, recv_sem=recv_sem,
            device_id=device, device_id_type=MESH,
        )

    for name in ("current", "weight", "route_v", "slot_v"):
        loads[name].wait()
    leaf_row = route_v[...] * LEAVES + slot_v[...]
    leaf_count = SUB * LEAVES
    hot = (
        lax.broadcasted_iota(jnp.int32, (leaf_count, PATCHES), 0)
        == jnp.broadcast_to(leaf_row, (leaf_count, PATCHES))
    ).astype(F32).astype(BF16)
    scaled_weight = weight[...] * SCALE

    def leaf_sums(read, store):
        for r in range(0, RHS, 2):
            pair = [(read(pl.ds(r + i, PATCHES, stride=RHS)) * scaled_weight).astype(BF16) for i in range(2)]
            sums = dot(hot, jnp.concatenate(pair, axis=1))
            for t in range(SUB):
                rows = slice(t * LEAVES, (t + 1) * LEAVES)
                tile = jnp.concatenate([sums[rows, :NODES], sums[rows, NODES:]], axis=0)
                store(t, slice(r * LEAVES, (r + 2) * LEAVES), tile.astype(BF16))

    def store1(t, rows, tile):
        send1[t, rows, :] = tile

    leaf_sums(lambda rows: basis[last, rows, :], store1)

    pl.semaphore_wait(barrier, len(peers))
    copies1 = start_all([
        remote(send1.at[t], recv1.at[d], s1.at[d], r1.at[d], (w, t)) for d, t in enumerate(subs)
    ])

    loads["edge0"].wait()
    loads["edge1"].wait()
    edge_send[0] = dot(basis[last, 0:RHS, :].astype(BF16), edge_corr[0])
    edge_send[1] = dot(basis[last, ROWS - RHS:, :].astype(BF16), edge_corr[1])
    edges = start_all([
        remote(edge_send.at[0], edge_recv.at[0], edge_s.at[0], edge_r.at[0], below_id),
        remote(edge_send.at[1], edge_recv.at[1], edge_s.at[1], edge_r.at[1], above_id),
    ])

    loads["multi"].wait()
    loads["up"].wait()

    def compose_up(leaf, carry):
        high, low = split(up[leaf])
        product = dot(multi[...], high) + dot(multi[...], low)
        rows = pl.ds(pl.multiple_of(leaf * NODES, NODES), NODES)
        up_high[rows, :], up_low[rows, :] = split(product)
        return carry

    lax.fori_loop(0, LEAVES, compose_up, 0)

    def half(p):
        return basis[last, patch_rows(p), :].astype(BF16)

    def near_pair(h, carry):
        p = 2 * h + 1
        left = jnp.concatenate([half(p), half(p + 1)], axis=1)
        right = jnp.concatenate(
            [
                jnp.concatenate([corr[3 * p + 1], corr[3 * p + 2]], axis=1),
                jnp.concatenate([corr[3 * p + 3], corr[3 * p + 4]], axis=1),
            ],
            axis=0,
        )
        both = dot(left, right)
        image[patch_rows(p), :] = both[:, :NODES] + dot(half(p - 1), corr[3 * p - 1])
        image[patch_rows(p + 1), :] = both[:, NODES:] + dot(half(p + 2), corr[3 * p + 6])
        return carry

    chunk = PATCHES // NEAR_CHUNKS // 2

    def near_chunk(c):
        corr_loads[c].wait()
        lax.fori_loop(max(0, c * chunk - 1), (c + 1) * chunk - 1, near_pair, 0, unroll=5 if c == 0 else 8)

    def bulk_store(j):
        def store(t, rows, tile):
            bulk_send[t % 2, t // 2, j, rows, :] = tile

        return store

    loads["basis"].wait()
    for j in range(last):
        leaf_sums(functools.partial(lambda k, rows: basis[k, rows, :], j), bulk_store(j))
    area_high, area_low = split(weight[...])
    areas = dot(hot, area_high) + dot(hot, area_low)
    for t in range(SUB):
        area_send[t] = areas[t * LEAVES:(t + 1) * LEAVES]
    early = pl.ds(0, last)
    pair_early = remote(
        bulk_send.at[1 - core, :, early], pair_recv.at[:, early], pair_s.at[0], pair_r.at[0], sibling
    )
    pair_early.start()
    near_chunk(0)
    near_chunk(1)

    for copy in copies1:
        copy.wait_recv()
    total = send1[s].astype(F32)
    for d in range(SUB - 1):
        total = total + recv1[d].astype(F32)
    sums1[...] = total
    lanes = jnp.concatenate(
        [sums1[pl.ds(leaf, RHS, stride=LEAVES), :] for leaf in range(LEAVES)], axis=1
    )
    tree = split_dot(lanes, up_high, up_low)
    send2[0] = tree[:, :NODES]
    send2[1] = tree[:, NODES:]
    copies2 = start_all([
        remote(send2.at[t // 4], recv2.at[d], s2.at[d], r2.at[d], (w, t)) for d, t in enumerate(subs)
    ])

    def pair_add(j):
        for t in range(SUB // 2):
            both = bulk_send[core, t, j].astype(F32) + pair_recv[t, j].astype(F32)
            pair_sums[t, j] = both.astype(BF16)

    pair_early.wait_recv()
    for j in range(last):
        pair_add(j)
    copies8 = start_all([
        remote(
            pair_sums.at[t, early], bulk_recv.at[d, early], s8.at[d], r8.at[d], (w, 2 * t + core)
        )
        for t, d in columns_z
    ] + [
        remote(area_send.at[t], area_recv.at[d], s9.at[d], r9.at[d], (w, t)) for d, t in enumerate(subs)
    ])

    loads["far"].wait()
    far_high[...], far_low[...] = split(far[...])
    near_chunk(2)
    near_chunk(3)
    for copy in edges:
        copy.wait()

    def current_half(p):
        return basis[last, p * RHS:(p + 1) * RHS, :].astype(BF16)

    from_below = jnp.where(me > 0, edge_recv[1], 0.0)
    from_above = jnp.where(me < WIDE * SUB - 1, edge_recv[0], 0.0)
    end = PATCHES - 1
    image[0:RHS, :] = (
        dot(current_half(0), corr[1]) + dot(current_half(1), corr[3]) + from_below
    )
    image[end * RHS:, :] = (
        dot(current_half(end), corr[3 * end + 1])
        + dot(current_half(end - 1), corr[3 * end - 1])
        + from_above
    )
    leaf_sums(lambda rows: image[rows, :], bulk_store(last))
    pair_late = remote(
        bulk_send.at[1 - core, :, last], pair_recv.at[:, last], pair_s.at[1], pair_r.at[1], sibling
    )
    pair_late.start()
    for copy in copies1:
        copy.wait_send()

    for copy in copies2:
        copy.wait_recv()
    half_tree = send2[s // 4]
    for d in range(SUB - 1):
        half_tree = half_tree + recv2[d]
    lane = lax.broadcasted_iota(jnp.int32, (RHS, NODES), 1)
    mine = jnp.where(lane // SHARE == lax.rem(s, 4), half_tree, 0.0)
    turn = lax.rem(lax.rem(w, 4) + 4 - lax.rem(s, 4), 4)
    placed = mine
    for k in range(1, 4):
        placed = jnp.where(turn == k, pltpu.roll(mine, k * SHARE, 1), placed)
    send3[...] = placed
    copies3 = start_all([
        remote(send3, recv3.at[w], s3.at[d], r3.at[w], (v, s)) for d, v in enumerate(wides)
    ])
    recv3[w] = placed

    pair_late.wait_recv()
    pair_add(last)
    copies10 = start_all([
        remote(pair_sums.at[t, last], bulk_recv.at[d, last], s10.at[d], r10.at[d], (w, 2 * t + core))
        for t, d in columns_z
    ])

    loads["eval"].wait()
    loads["down"].wait()

    def compose_down(leaf, carry):
        high, low = split(down[leaf])
        product = dot(high, evalm[...]) + dot(low, evalm[...])
        columns = pl.ds(pl.multiple_of(leaf * NODES, NODES), NODES)
        down_high[:, columns], down_low[:, columns] = split(product)
        return carry

    lax.fori_loop(0, LEAVES, compose_down, 0)
    zero = jnp.zeros((RHS, NODES), F32)

    def node_weight(p):
        return jnp.broadcast_to(weight[pl.ds(p, 1), :], (RHS, NODES))

    def gram_body(p, sums):
        rows = patch_rows(p)
        vectors = [basis[j, rows, :] for j in range(BASIS)]
        weighted = [v * node_weight(p) for v in vectors]
        return tuple(a + weighted[j] * vectors[k] for a, (j, k) in zip(sums, PAIRS))

    gram = lax.fori_loop(0, PATCHES, gram_body, (zero,) * len(PAIRS), unroll=2)
    packed = zero
    for i, value in enumerate(gram):
        packed = jnp.where(lane == BASIS + 1 + i, jnp.sum(value, axis=1, keepdims=True), packed)
    for copy in copies2:
        copy.wait_send()

    for d, v in enumerate(wide_sources):
        remote(send3, recv3.at[v], s3.at[d], r3.at[v], (v, s)).wait_recv()
    lanes = jnp.concatenate(
        [
            (recv3[4 * g] + recv3[4 * g + 1]) + (recv3[4 * g + 2] + recv3[4 * g + 3])
            for g in range(WIDE // 4)
        ],
        axis=1,
    )
    send4[...] = split_dot(lanes, far_high, far_low)
    copies4 = start_all([
        remote(send4, recv4.at[d], s4.at[d], r4.at[d], (w, t)) for d, t in enumerate(subs)
    ])

    def near_products(p, sums):
        rows = patch_rows(p)
        value = image[rows, :]
        weighted = value * node_weight(p)
        return tuple(
            a + weighted * (basis[i, rows, :] if i < BASIS else value) for i, a in enumerate(sums)
        )

    products = lax.fori_loop(0, PATCHES, near_products, (zero,) * (BASIS + 1), unroll=2)
    for copy in copies3:
        copy.wait_send()
    for copy in copies8 + copies10:
        copy.wait_recv()
    for j in range(BASIS):
        total = pair_sums[s // 2, j].astype(F32)
        for d in range(SUB // 2 - 1):
            total = total + bulk_recv[d, j].astype(F32)
        bulk_sums[j] = total
    area = area_send[s]
    for d in range(SUB - 1):
        area = area + area_recv[d]

    for copy in copies4:
        copy.wait_recv()
    local = send4[...]
    for d in range(SUB - 1):
        local = local + recv4[d]
    potentials = split_dot(local, down_high, down_low).astype(BF16)
    far_sums = [zero] * (BASIS + 2)
    for leaf in range(LEAVES):
        field[s * LEAVES + leaf] = potentials[:, leaf * NODES:(leaf + 1) * NODES]
        value = potentials[:, leaf * NODES:(leaf + 1) * NODES].astype(F32)
        rows = pl.ds(leaf, RHS, stride=LEAVES)
        others = [bulk_sums[j, rows, :] for j in range(last)]
        others += [sums1[rows, :], bulk_sums[last, rows, :]]
        others += [value * jnp.broadcast_to(area[leaf:leaf + 1], (RHS, NODES))]
        far_sums = [a + value * b for a, b in zip(far_sums, others)]
    products = [products[j] + far_sums[j] * (1.0 / SCALE) for j in range(BASIS)] + [
        products[BASIS] + far_sums[BASIS] * (2.0 / SCALE) + far_sums[BASIS + 1]
    ]
    for i, value in enumerate(products):
        packed = jnp.where(lane == i, jnp.sum(value, axis=1, keepdims=True), packed)
    low_rows = RHS // 2
    share = packed[:low_rows] + pltpu.roll(packed[low_rows:], RHS, 1)
    send7[...] = share
    copies7 = start_all([
        remote(send7, recv7.at[w], s7.at[d], r7.at[w], (v, s)) for d, v in enumerate(wides)
    ])
    recv7[w] = share
    own = pl.ds(s * LEAVES, LEAVES)
    copies5 = start_all([
        remote(field.at[own], field.at[own], s5.at[d], r5.at[s], (w, t)) for d, t in enumerate(subs)
    ])
    for name in ("route_s", "slot_s"):
        loads[name].wait()
    for copy in copies4 + copies8 + copies10 + [pair_early, pair_late]:
        copy.wait_send()

    for d, v in enumerate(wide_sources):
        remote(send7, recv7.at[v], s7.at[d], r7.at[v], (v, s)).wait_recv()
    total7 = recv7[0]
    for v in range(1, WIDE):
        total7 = total7 + recv7[v]
    send6[...] = total7
    copies6 = start_all([
        remote(send6, recv6.at[s], s6.at[d], r6.at[s], (w, t)) for d, t in enumerate(subs)
    ])
    recv6[s] = total7

    for d in range(1, SUB):
        t = lax.rem(s + SUB - d, SUB)
        block = field.at[pl.ds(t * LEAVES, LEAVES)]
        remote(block, block, s5.at[d - 1], r5.at[t], (w, t)).wait_recv()

    def add_far(p, carry):
        rows = patch_rows(p)
        leaf = route_s[0, p] * LEAVES + slot_s[0, p]
        image[rows, :] = image[rows, :] + field[leaf].astype(F32)
        return carry

    lax.fori_loop(0, PATCHES, add_far, 0, unroll=4)
    for copy in copies5 + copies7:
        copy.wait_send()
    for d in range(1, SUB):
        t = lax.rem(s + SUB - d, SUB)
        remote(send6, recv6.at[t], s6.at[d - 1], r6.at[t], (w, t)).wait_recv()
    total7 = recv6[0]
    for t in range(1, SUB):
        total7 = total7 + recv6[t]
    total7 = total7 * (1.0 / TOTAL)
    full = jnp.concatenate([total7, pltpu.roll(total7, NODES - RHS, 1)], axis=0)

    def column(i):
        return full[:, i:i + 1]

    gram_of = {}
    for i, (j, k) in enumerate(PAIRS):
        gram_of[j, k] = gram_of[k, j] = column(BASIS + 1 + i)
    fields = [column(j) for j in range(BASIS)]
    first = [fields[j] + 0.5 * gram_of[j, last] for j in range(BASIS)]
    coeffs = []
    for j in range(BASIS):
        second = first[j]
        for k in range(BASIS):
            second = second - gram_of[j, k] * first[k]
        coeffs.append(first[j] + second)
    deltas = [coeffs[j] - 0.5 if j == last else coeffs[j] for j in range(BASIS)]
    square = column(BASIS)
    for j in range(BASIS):
        inner = -2.0 * fields[j]
        for k in range(BASIS):
            inner = inner + gram_of[j, k] * deltas[k]
        square = square + deltas[j] * inner
    beta = jnp.sqrt(jnp.maximum(square, 0.0) + 1e-6)
    inverse = jnp.broadcast_to(1.0 / beta, (RHS, NODES))
    factors = [jnp.broadcast_to(value, (RHS, NODES)) * inverse for value in deltas]

    def final_body(p, carry):
        rows = patch_rows(p)
        value = image[rows, :] * inverse
        for j in range(BASIS):
            value = value - factors[j] * basis[j, rows, :]
        vector_out[rows, :] = value
        return carry

    lax.fori_loop(0, PATCHES, final_body, 0, unroll=4)
    row = lax.broadcasted_iota(jnp.int32, (RHS, NODES), 0)
    columns = coeffs + [beta]
    for i, value in enumerate(columns):
        flat = jnp.sum(jnp.where(row == lane, value, 0.0), axis=0, keepdims=True)
        hess_out[i:i + 1, :] = flat[:, :RHS]
    for copy in copies6:
        copy.wait_send()


def per_device(
    krylov_basis, quad_weight, corrections, patch_route, leaf_slot, multipole_map,
    upward_translation, far_coupling, downward_translation, evaluation_map,
):
    outside = pl.BlockSpec(memory_space=pl.ANY)
    inside = pl.BlockSpec(memory_space=pltpu.VMEM)
    dma = pltpu.SemaphoreType.DMA
    near_blocks = 3 * PATCHES
    vector, hessenberg = pl.pallas_call(
        kernel,
        out_shape=(
            pltpu.VMEM((ROWS, NODES), F32),
            pltpu.VMEM((BASIS + 1, RHS), F32),
        ),
        in_specs=[outside] * 10,
        out_specs=(inside, inside),
        scratch_shapes=[
            pltpu.VMEM((BASIS, ROWS, NODES), F32),
            pltpu.VMEM((PATCHES, NODES), F32),
            pltpu.VMEM((near_blocks, NODES, NODES), BF16),
            pltpu.VMEM((1, PATCHES), jnp.int32),
            pltpu.VMEM((1, PATCHES), jnp.int32),
            pltpu.SMEM((1, PATCHES), jnp.int32),
            pltpu.SMEM((1, PATCHES), jnp.int32),
            pltpu.VMEM((NODES, COEFFS), BF16),
            pltpu.VMEM((LEAVES, COEFFS, COEFFS), F32),
            pltpu.VMEM((WIDE * SHARE, COEFFS), F32),
            pltpu.VMEM((LEAVES, COEFFS, COEFFS), F32),
            pltpu.VMEM((COEFFS, NODES), BF16),
            pltpu.VMEM((2, NODES, NODES), BF16),
            pltpu.VMEM((LEAVES * NODES, COEFFS), BF16),
            pltpu.VMEM((LEAVES * NODES, COEFFS), BF16),
            pltpu.VMEM((WIDE * SHARE, COEFFS), BF16),
            pltpu.VMEM((WIDE * SHARE, COEFFS), BF16),
            pltpu.VMEM((COEFFS, LEAVES * NODES), BF16),
            pltpu.VMEM((COEFFS, LEAVES * NODES), BF16),
            pltpu.VMEM((ROWS, NODES), F32),
            pltpu.VMEM((SUB, RHS * LEAVES, NODES), BF16),
            pltpu.VMEM((SUB - 1, RHS * LEAVES, NODES), BF16),
            pltpu.VMEM((RHS * LEAVES, NODES), F32),
            pltpu.VMEM((2, RHS, NODES), F32),
            pltpu.VMEM((SUB - 1, RHS, NODES), F32),
            pltpu.VMEM((RHS, NODES), F32),
            pltpu.VMEM((WIDE, RHS, NODES), F32),
            pltpu.VMEM((RHS, COEFFS), F32),
            pltpu.VMEM((SUB - 1, RHS, COEFFS), F32),
            pltpu.VMEM((SUB * LEAVES, RHS, NODES), BF16),
            pltpu.VMEM((2, RHS, NODES), F32),
            pltpu.VMEM((2, RHS, NODES), F32),
            pltpu.VMEM((RHS // 2, NODES), F32),
            pltpu.VMEM((SUB, RHS // 2, NODES), F32),
            pltpu.VMEM((RHS // 2, NODES), F32),
            pltpu.VMEM((WIDE, RHS // 2, NODES), F32),
            pltpu.VMEM((2, SUB // 2, BASIS, RHS * LEAVES, NODES), BF16),
            pltpu.VMEM((SUB // 2, BASIS, RHS * LEAVES, NODES), BF16),
            pltpu.VMEM((SUB // 2, BASIS, RHS * LEAVES, NODES), BF16),
            pltpu.VMEM((SUB // 2 - 1, BASIS, RHS * LEAVES, NODES), BF16),
            pltpu.VMEM((BASIS, RHS * LEAVES, NODES), F32),
            pltpu.VMEM((SUB, LEAVES, NODES), F32),
            pltpu.VMEM((SUB - 1, LEAVES, NODES), F32),
            dma((16,)), dma((NEAR_CHUNKS,)), dma((2,)), dma((2,)),
            dma((SUB - 1,)), dma((SUB - 1,)),
            dma((SUB - 1,)), dma((SUB - 1,)),
            dma((WIDE - 1,)), dma((WIDE,)),
            dma((SUB - 1,)), dma((SUB - 1,)),
            dma((SUB - 1,)), dma((SUB,)),
            dma((SUB - 1,)), dma((SUB,)),
            dma((WIDE - 1,)), dma((WIDE,)),
            dma((SUB // 2 - 1,)), dma((SUB // 2 - 1,)),
            dma((SUB - 1,)), dma((SUB - 1,)),
            dma((SUB // 2 - 1,)), dma((SUB // 2 - 1,)),
            dma((2,)), dma((2,)),
        ],
        compiler_params=pltpu.CompilerParams(
            collective_id=0, has_side_effects=True, vmem_limit_bytes=60 << 20
        ),
    )(
        krylov_basis.reshape(BASIS, ROWS, NODES),
        quad_weight,
        corrections.reshape(near_blocks, NODES, NODES),
        patch_route.reshape(1, PATCHES),
        leaf_slot.reshape(1, PATCHES),
        multipole_map,
        upward_translation,
        far_coupling.reshape(WIDE * SHARE, COEFFS),
        downward_translation,
        evaluation_map,
    )
    return vector.reshape(PATCHES, RHS, NODES), hessenberg


def solution(mesh):
    return jax.shard_map(
        per_device,
        mesh=mesh,
        in_specs=(
            P(None, ("wide", "sub"), None, None),
            P(("wide", "sub"), None),
            P(("wide", "sub"), None, None, None),
            P(("wide", "sub"), None),
            P(("wide", "sub")),
            P(),
            P(("wide", "sub"), None, None),
            P("wide", None, "sub", None),
            P(("wide", "sub"), None, None),
            P(),
        ),
        out_specs=(P(("wide", "sub"), None, None), P()),
        check_vma=False,
    )
```

```python
import functools

import jax
import jax.numpy as jnp
from jax import lax
from jax.experimental import pallas as pl
from jax.experimental.pallas import tpu as pltpu
from jax.sharding import PartitionSpec as P

MESH = pl.DeviceIdType.MESH
F32 = jnp.float32
BF16 = jnp.bfloat16
WIDE, SUB = 16, 8
PATCHES, RHS, NODES, COEFFS, BASIS, LEAVES = 128, 16, 128, 256, 4, 8
SHARE = COEFFS // SUB
ROWS = PATCHES * RHS
TOTAL = float(WIDE * SUB * PATCHES * NODES)
SCALE = 1.0 / 32.0
PACK = NODES // RHS
DEVICES = WIDE * SUB
PAIRS = [(j, k) for j in range(BASIS) for k in range(j, BASIS)]
NEAR_CHUNKS = 4


def split(value):
    high = value.astype(BF16)
    return high, (value - high.astype(F32)).astype(BF16)


def dot(a, b):
    return jnp.dot(a, b, preferred_element_type=F32)


def split_dot(value, high_ref, low_ref):
    high, low = split(value)
    rows = value.shape[0]
    both = dot(jnp.concatenate([high, low], axis=0), high_ref[...])
    return both[:rows] + both[rows:] + dot(high, low_ref[...])


def patch_rows(p):
    return pl.ds(pl.multiple_of(p * RHS, RHS), RHS)


def kernel(
    basis_hbm, weight_hbm, corr_hbm, route_hbm, slot_hbm, multi_hbm, up_hbm, far_hbm, down_hbm,
    eval_hbm, vector_out, hess_out,
    basis, weight, corr, route_v, slot_v, route_s, slot_s, multi, up, far, down, evalm, edge_corr,
    up_high, up_low, far_high, far_low, down_high, down_low, image,
    send1, recv1, sums1, send2, recv2, send3, recv3, send4, recv4, field,
    edge_send, edge_recv, send7, recv7, bulk_send, pair_recv, pair_sums, bulk_recv, bulk_sums, area_send, area_recv,
    load_sem, corr_sem, edge_s, edge_r, s1, r1, s2, r2, s3, r3, s4, r4, s5, r5, s7, r7,
    s8, r8, s9, r9, s10, r10, pair_s, pair_r,
):
    w = lax.axis_index("wide")
    s = lax.axis_index("sub")
    me = w * SUB + s
    below = lax.rem(me + WIDE * SUB - 1, WIDE * SUB)
    above = lax.rem(me + 1, WIDE * SUB)
    below_id = (below // SUB, lax.rem(below, SUB))
    above_id = (above // SUB, lax.rem(above, SUB))
    subs = [lax.rem(s + d, SUB) for d in range(1, SUB)]
    core = lax.rem(s, 2)
    sibling = (w, s + 1 - 2 * core)
    columns_z = [(lax.rem(s // 2 + d, SUB // 2), d - 1) for d in range(1, SUB // 2)]
    wides = [lax.rem(w + d, WIDE) for d in range(1, WIDE)]
    wide_sources = [lax.rem(w + WIDE - d, WIDE) for d in range(1, WIDE)]

    barrier = pltpu.get_barrier_semaphore()
    peers = [(w, t) for t in subs] + [(v, s) for v in wides] + [below_id, above_id]
    for peer in peers:
        pl.semaphore_signal(barrier, inc=1, device_id=peer, device_id_type=MESH)

    last = BASIS - 1
    loads = {}

    def load(name, source, target):
        copy = pltpu.make_async_copy(source, target, load_sem.at[len(loads)])
        copy.start()
        loads[name] = copy

    load("current", basis_hbm.at[last], basis.at[last])
    load("weight", weight_hbm, weight)
    load("route_v", route_hbm, route_v)
    load("slot_v", slot_hbm, slot_v)
    load("multi", multi_hbm, multi)
    load("up", up_hbm, up)
    load("edge0", corr_hbm.at[0], edge_corr.at[0])
    load("edge1", corr_hbm.at[3 * PATCHES - 1], edge_corr.at[1])
    load("basis", basis_hbm.at[pl.ds(0, last)], basis.at[pl.ds(0, last)])
    load("route_s", route_hbm, route_s)
    load("slot_s", slot_hbm, slot_s)
    blocks = 3 * PATCHES // NEAR_CHUNKS
    corr_loads = []
    for c in range(NEAR_CHUNKS):
        copy = pltpu.make_async_copy(
            corr_hbm.at[pl.ds(c * blocks, blocks)], corr.at[pl.ds(c * blocks, blocks)], corr_sem.at[c]
        )
        copy.start()
        corr_loads.append(copy)
    load("far", far_hbm, far)
    load("eval", eval_hbm, evalm)
    load("down", down_hbm, down)

    def start_all(copies):
        for copy in copies:
            copy.start()
        return copies

    def remote(source, target, send_sem, recv_sem, device):
        return pltpu.make_async_remote_copy(
            src_ref=source, dst_ref=target, send_sem=send_sem, recv_sem=recv_sem,
            device_id=device, device_id_type=MESH,
        )

    for name in ("current", "weight", "route_v", "slot_v"):
        loads[name].wait()
    leaf_row = route_v[...] * LEAVES + slot_v[...]
    leaf_count = SUB * LEAVES
    hot = (
        lax.broadcasted_iota(jnp.int32, (leaf_count, PATCHES), 0)
        == jnp.broadcast_to(leaf_row, (leaf_count, PATCHES))
    ).astype(F32).astype(BF16)
    scaled_weight = weight[...] * SCALE

    def leaf_sums(read, store):
        for r in range(0, RHS, 2):
            pair = [(read(pl.ds(r + i, PATCHES, stride=RHS)) * scaled_weight).astype(BF16) for i in range(2)]
            sums = dot(hot, jnp.concatenate(pair, axis=1))
            for t in range(SUB):
                rows = slice(t * LEAVES, (t + 1) * LEAVES)
                tile = jnp.concatenate([sums[rows, :NODES], sums[rows, NODES:]], axis=0)
                store(t, slice(r * LEAVES, (r + 2) * LEAVES), tile.astype(BF16))

    def store1(t, rows, tile):
        send1[t, rows, :] = tile

    leaf_sums(lambda rows: basis[last, rows, :], store1)

    pl.semaphore_wait(barrier, len(peers))
    copies1 = start_all([
        remote(send1.at[t], recv1.at[d], s1.at[d], r1.at[d], (w, t)) for d, t in enumerate(subs)
    ])

    loads["edge0"].wait()
    loads["edge1"].wait()
    edge_send[0] = dot(basis[last, 0:RHS, :].astype(BF16), edge_corr[0])
    edge_send[1] = dot(basis[last, ROWS - RHS:, :].astype(BF16), edge_corr[1])
    edges = start_all([
        remote(edge_send.at[0], edge_recv.at[0], edge_s.at[0], edge_r.at[0], below_id),
        remote(edge_send.at[1], edge_recv.at[1], edge_s.at[1], edge_r.at[1], above_id),
    ])

    loads["multi"].wait()
    loads["up"].wait()

    def compose_up(leaf, carry):
        high, low = split(up[leaf])
        product = dot(multi[...], high) + dot(multi[...], low)
        rows = pl.ds(pl.multiple_of(leaf * NODES, NODES), NODES)
        up_high[rows, :], up_low[rows, :] = split(product)
        return carry

    lax.fori_loop(0, LEAVES, compose_up, 0)

    def half(p):
        return basis[last, patch_rows(p), :].astype(BF16)

    def near_pair(h, carry):
        p = 2 * h + 1
        left = jnp.concatenate([half(p), half(p + 1)], axis=1)
        right = jnp.concatenate(
            [
                jnp.concatenate([corr[3 * p + 1], corr[3 * p + 2]], axis=1),
                jnp.concatenate([corr[3 * p + 3], corr[3 * p + 4]], axis=1),
            ],
            axis=0,
        )
        both = dot(left, right)
        image[patch_rows(p), :] = both[:, :NODES] + dot(half(p - 1), corr[3 * p - 1])
        image[patch_rows(p + 1), :] = both[:, NODES:] + dot(half(p + 2), corr[3 * p + 6])
        return carry

    chunk = PATCHES // NEAR_CHUNKS // 2

    def near_chunk(c):
        corr_loads[c].wait()
        lax.fori_loop(max(0, c * chunk - 1), (c + 1) * chunk - 1, near_pair, 0, unroll=5 if c == 0 else 8)

    def bulk_store(j):
        def store(t, rows, tile):
            bulk_send[t % 2, t // 2, j, rows, :] = tile

        return store

    loads["basis"].wait()
    for j in range(last):
        leaf_sums(functools.partial(lambda k, rows: basis[k, rows, :], j), bulk_store(j))
    area_high, area_low = split(weight[...])
    areas = dot(hot, area_high) + dot(hot, area_low)
    for t in range(SUB):
        area_send[t] = areas[t * LEAVES:(t + 1) * LEAVES]
    early = pl.ds(0, last)
    pair_early = remote(
        bulk_send.at[1 - core, :, early], pair_recv.at[:, early], pair_s.at[0], pair_r.at[0], sibling
    )
    pair_early.start()
    near_chunk(0)
    near_chunk(1)

    for copy in copies1:
        copy.wait_recv()
    total = send1[s].astype(F32)
    for d in range(SUB - 1):
        total = total + recv1[d].astype(F32)
    sums1[...] = total
    lanes = jnp.concatenate(
        [sums1[pl.ds(leaf, RHS, stride=LEAVES), :] for leaf in range(LEAVES)], axis=1
    )
    tree = split_dot(lanes, up_high, up_low)
    send2[0] = tree[:, :NODES]
    send2[1] = tree[:, NODES:]
    copies2 = start_all([
        remote(send2.at[t // 4], recv2.at[d], s2.at[d], r2.at[d], (w, t)) for d, t in enumerate(subs)
    ])

    def pair_add(j):
        for t in range(SUB // 2):
            both = bulk_send[core, t, j].astype(F32) + pair_recv[t, j].astype(F32)
            pair_sums[t, j] = both.astype(BF16)

    pair_early.wait_recv()
    for j in range(last):
        pair_add(j)
    copies8 = start_all([
        remote(
            pair_sums.at[t, early], bulk_recv.at[d, early], s8.at[d], r8.at[d], (w, 2 * t + core)
        )
        for t, d in columns_z
    ] + [
        remote(area_send.at[t], area_recv.at[d], s9.at[d], r9.at[d], (w, t)) for d, t in enumerate(subs)
    ])

    loads["far"].wait()
    far_high[...], far_low[...] = split(far[...])
    near_chunk(2)
    near_chunk(3)
    for copy in edges:
        copy.wait()

    def current_half(p):
        return basis[last, p * RHS:(p + 1) * RHS, :].astype(BF16)

    from_below = jnp.where(me > 0, edge_recv[1], 0.0)
    from_above = jnp.where(me < WIDE * SUB - 1, edge_recv[0], 0.0)
    end = PATCHES - 1
    image[0:RHS, :] = (
        dot(current_half(0), corr[1]) + dot(current_half(1), corr[3]) + from_below
    )
    image[end * RHS:, :] = (
        dot(current_half(end), corr[3 * end + 1])
        + dot(current_half(end - 1), corr[3 * end - 1])
        + from_above
    )
    leaf_sums(lambda rows: image[rows, :], bulk_store(last))
    pair_late = remote(
        bulk_send.at[1 - core, :, last], pair_recv.at[:, last], pair_s.at[1], pair_r.at[1], sibling
    )
    pair_late.start()
    for copy in copies1:
        copy.wait_send()

    for copy in copies2:
        copy.wait_recv()
    half_tree = send2[s // 4]
    for d in range(SUB - 1):
        half_tree = half_tree + recv2[d]
    lane = lax.broadcasted_iota(jnp.int32, (RHS, NODES), 1)
    mine = jnp.where(lane // SHARE == lax.rem(s, 4), half_tree, 0.0)
    turn = lax.rem(lax.rem(w, 4) + 4 - lax.rem(s, 4), 4)
    placed = mine
    for k in range(1, 4):
        placed = jnp.where(turn == k, pltpu.roll(mine, k * SHARE, 1), placed)
    send3[...] = placed
    copies3 = start_all([
        remote(send3, recv3.at[w], s3.at[d], r3.at[w], (v, s)) for d, v in enumerate(wides)
    ])
    recv3[w] = placed

    pair_late.wait_recv()
    pair_add(last)
    copies10 = start_all([
        remote(pair_sums.at[t, last], bulk_recv.at[d, last], s10.at[d], r10.at[d], (w, 2 * t + core))
        for t, d in columns_z
    ])

    loads["eval"].wait()
    loads["down"].wait()

    def compose_down(leaf, carry):
        high, low = split(down[leaf])
        product = dot(high, evalm[...]) + dot(low, evalm[...])
        columns = pl.ds(pl.multiple_of(leaf * NODES, NODES), NODES)
        down_high[:, columns], down_low[:, columns] = split(product)
        return carry

    lax.fori_loop(0, LEAVES, compose_down, 0)
    zero = jnp.zeros((RHS, NODES), F32)

    def node_weight(p):
        return jnp.broadcast_to(weight[pl.ds(p, 1), :], (RHS, NODES))

    def gram_body(p, sums):
        rows = patch_rows(p)
        vectors = [basis[j, rows, :] for j in range(BASIS)]
        weighted = [v * node_weight(p) for v in vectors]
        return tuple(a + weighted[j] * vectors[k] for a, (j, k) in zip(sums, PAIRS))

    gram = lax.fori_loop(0, PATCHES, gram_body, (zero,) * len(PAIRS), unroll=2)
    row = lax.broadcasted_iota(jnp.int32, (RHS, NODES), 0)
    spots = [(lane // RHS == m) & (lane % RHS == row) for m in range(PACK)]

    def pack(tiles, first, values):
        tiles = list(tiles)
        for i, value in enumerate(values, first):
            total = jnp.sum(value, axis=1, keepdims=True)
            tiles[i // PACK] = jnp.where(spots[i % PACK], total, tiles[i // PACK])
        return tiles

    packed = pack([zero, zero], BASIS + 1, gram)
    for copy in copies2:
        copy.wait_send()

    for d, v in enumerate(wide_sources):
        remote(send3, recv3.at[v], s3.at[d], r3.at[v], (v, s)).wait_recv()
    lanes = jnp.concatenate(
        [
            (recv3[4 * g] + recv3[4 * g + 1]) + (recv3[4 * g + 2] + recv3[4 * g + 3])
            for g in range(WIDE // 4)
        ],
        axis=1,
    )
    send4[...] = split_dot(lanes, far_high, far_low)
    copies4 = start_all([
        remote(send4, recv4.at[d], s4.at[d], r4.at[d], (w, t)) for d, t in enumerate(subs)
    ])

    def near_products(p, sums):
        rows = patch_rows(p)
        value = image[rows, :]
        weighted = value * node_weight(p)
        return tuple(
            a + weighted * (basis[i, rows, :] if i < BASIS else value) for i, a in enumerate(sums)
        )

    products = lax.fori_loop(0, PATCHES, near_products, (zero,) * (BASIS + 1), unroll=2)
    for copy in copies3:
        copy.wait_send()
    for copy in copies8 + copies10:
        copy.wait_recv()
    for j in range(BASIS):
        total = pair_sums[s // 2, j].astype(F32)
        for d in range(SUB // 2 - 1):
            total = total + bulk_recv[d, j].astype(F32)
        bulk_sums[j] = total
    area = area_send[s]
    for d in range(SUB - 1):
        area = area + area_recv[d]

    for copy in copies4:
        copy.wait_recv()
    local = send4[...]
    for d in range(SUB - 1):
        local = local + recv4[d]
    potentials = split_dot(local, down_high, down_low).astype(BF16)
    far_sums = [zero] * (BASIS + 2)
    for leaf in range(LEAVES):
        field[s * LEAVES + leaf] = potentials[:, leaf * NODES:(leaf + 1) * NODES]
        value = potentials[:, leaf * NODES:(leaf + 1) * NODES].astype(F32)
        rows = pl.ds(leaf, RHS, stride=LEAVES)
        others = [bulk_sums[j, rows, :] for j in range(last)]
        others += [sums1[rows, :], bulk_sums[last, rows, :]]
        others += [value * jnp.broadcast_to(area[leaf:leaf + 1], (RHS, NODES))]
        far_sums = [a + value * b for a, b in zip(far_sums, others)]
    products = [products[j] + far_sums[j] * (1.0 / SCALE) for j in range(BASIS)] + [
        products[BASIS] + far_sums[BASIS] * (2.0 / SCALE) + far_sums[BASIS + 1]
    ]
    packed = pack(packed, 0, products)
    for a in range(2):
        send7[a:a + 1, :] = jnp.sum(packed[a], axis=0, keepdims=True)

    own = pl.ds(s * LEAVES, LEAVES)
    copies5 = start_all([
        remote(field.at[own], field.at[own], s5.at[d], r5.at[s], (w, t)) for d, t in enumerate(subs)
    ])

    def share(v, t):
        return remote(send7, recv7.at[me], s7.at[0], r7.at[0], (v, t))

    def share_wide(d, carry):
        v = lax.rem(w + d, WIDE)
        for e in range(SUB):
            share(v, lax.rem(s + e, SUB)).start()
        return carry

    lax.fori_loop(1, WIDE, share_wide, 0)
    for t in subs:
        share(w, t).start()
    recv7[me] = send7[...]
    for name in ("route_s", "slot_s"):
        loads[name].wait()
    for copy in copies4 + copies8 + copies10 + [pair_early, pair_late]:
        copy.wait_send()

    for d in range(1, SUB):
        t = lax.rem(s + SUB - d, SUB)
        block = field.at[pl.ds(t * LEAVES, LEAVES)]
        remote(block, block, s5.at[d - 1], r5.at[t], (w, t)).wait_recv()

    def add_far(p, carry):
        rows = patch_rows(p)
        leaf = route_s[0, p] * LEAVES + slot_s[0, p]
        image[rows, :] = image[rows, :] + field[leaf].astype(F32)
        return carry

    lax.fori_loop(0, PATCHES, add_far, 0, unroll=4)
    for copy in copies5:
        copy.wait_send()
    others = recv7.at[pl.ds(0, DEVICES - 1)]
    everyone = remote(others, others, s7.at[0], r7.at[0], sibling)
    everyone.wait_recv()
    totals = jnp.sum(recv7[...], axis=0) * (1.0 / TOTAL)
    wholes = [jnp.broadcast_to(totals[a:a + 1], (RHS, NODES)) for a in range(2)]

    def column(i):
        return jnp.sum(jnp.where(spots[i % PACK], wholes[i // PACK], 0.0), axis=1, keepdims=True)

    gram_of = {}
    for i, (j, k) in enumerate(PAIRS):
        gram_of[j, k] = gram_of[k, j] = column(BASIS + 1 + i)
    fields = [column(j) for j in range(BASIS)]
    first = [fields[j] + 0.5 * gram_of[j, last] for j in range(BASIS)]
    coeffs = []
    for j in range(BASIS):
        second = first[j]
        for k in range(BASIS):
            second = second - gram_of[j, k] * first[k]
        coeffs.append(first[j] + second)
    deltas = [coeffs[j] - 0.5 if j == last else coeffs[j] for j in range(BASIS)]
    square = column(BASIS)
    for j in range(BASIS):
        inner = -2.0 * fields[j]
        for k in range(BASIS):
            inner = inner + gram_of[j, k] * deltas[k]
        square = square + deltas[j] * inner
    beta = jnp.sqrt(jnp.maximum(square, 0.0) + 1e-6)
    inverse = jnp.broadcast_to(1.0 / beta, (RHS, NODES))
    factors = [jnp.broadcast_to(value, (RHS, NODES)) * inverse for value in deltas]

    def final_body(p, carry):
        rows = patch_rows(p)
        value = image[rows, :] * inverse
        for j in range(BASIS):
            value = value - factors[j] * basis[j, rows, :]
        vector_out[rows, :] = value
        return carry

    lax.fori_loop(0, PATCHES, final_body, 0, unroll=4)
    columns = coeffs + [beta]
    for i, value in enumerate(columns):
        flat = jnp.sum(jnp.where(row == lane, value, 0.0), axis=0, keepdims=True)
        hess_out[i:i + 1, :] = flat[:, :RHS]
    everyone.wait_send()


def per_device(
    krylov_basis, quad_weight, corrections, patch_route, leaf_slot, multipole_map,
    upward_translation, far_coupling, downward_translation, evaluation_map,
):
    outside = pl.BlockSpec(memory_space=pl.ANY)
    inside = pl.BlockSpec(memory_space=pltpu.VMEM)
    dma = pltpu.SemaphoreType.DMA
    near_blocks = 3 * PATCHES
    vector, hessenberg = pl.pallas_call(
        kernel,
        out_shape=(
            pltpu.VMEM((ROWS, NODES), F32),
            pltpu.VMEM((BASIS + 1, RHS), F32),
        ),
        in_specs=[outside] * 10,
        out_specs=(inside, inside),
        scratch_shapes=[
            pltpu.VMEM((BASIS, ROWS, NODES), F32),
            pltpu.VMEM((PATCHES, NODES), F32),
            pltpu.VMEM((near_blocks, NODES, NODES), BF16),
            pltpu.VMEM((1, PATCHES), jnp.int32),
            pltpu.VMEM((1, PATCHES), jnp.int32),
            pltpu.SMEM((1, PATCHES), jnp.int32),
            pltpu.SMEM((1, PATCHES), jnp.int32),
            pltpu.VMEM((NODES, COEFFS), BF16),
            pltpu.VMEM((LEAVES, COEFFS, COEFFS), F32),
            pltpu.VMEM((WIDE * SHARE, COEFFS), F32),
            pltpu.VMEM((LEAVES, COEFFS, COEFFS), F32),
            pltpu.VMEM((COEFFS, NODES), BF16),
            pltpu.VMEM((2, NODES, NODES), BF16),
            pltpu.VMEM((LEAVES * NODES, COEFFS), BF16),
            pltpu.VMEM((LEAVES * NODES, COEFFS), BF16),
            pltpu.VMEM((WIDE * SHARE, COEFFS), BF16),
            pltpu.VMEM((WIDE * SHARE, COEFFS), BF16),
            pltpu.VMEM((COEFFS, LEAVES * NODES), BF16),
            pltpu.VMEM((COEFFS, LEAVES * NODES), BF16),
            pltpu.VMEM((ROWS, NODES), F32),
            pltpu.VMEM((SUB, RHS * LEAVES, NODES), BF16),
            pltpu.VMEM((SUB - 1, RHS * LEAVES, NODES), BF16),
            pltpu.VMEM((RHS * LEAVES, NODES), F32),
            pltpu.VMEM((2, RHS, NODES), F32),
            pltpu.VMEM((SUB - 1, RHS, NODES), F32),
            pltpu.VMEM((RHS, NODES), F32),
            pltpu.VMEM((WIDE, RHS, NODES), F32),
            pltpu.VMEM((RHS, COEFFS), F32),
            pltpu.VMEM((SUB - 1, RHS, COEFFS), F32),
            pltpu.VMEM((SUB * LEAVES, RHS, NODES), BF16),
            pltpu.VMEM((2, RHS, NODES), F32),
            pltpu.VMEM((2, RHS, NODES), F32),
            pltpu.VMEM((2, NODES), F32),
            pltpu.VMEM((DEVICES, 2, NODES), F32),
            pltpu.VMEM((2, SUB // 2, BASIS, RHS * LEAVES, NODES), BF16),
            pltpu.VMEM((SUB // 2, BASIS, RHS * LEAVES, NODES), BF16),
            pltpu.VMEM((SUB // 2, BASIS, RHS * LEAVES, NODES), BF16),
            pltpu.VMEM((SUB // 2 - 1, BASIS, RHS * LEAVES, NODES), BF16),
            pltpu.VMEM((BASIS, RHS * LEAVES, NODES), F32),
            pltpu.VMEM((SUB, LEAVES, NODES), F32),
            pltpu.VMEM((SUB - 1, LEAVES, NODES), F32),
            dma((16,)), dma((NEAR_CHUNKS,)), dma((2,)), dma((2,)),
            dma((SUB - 1,)), dma((SUB - 1,)),
            dma((SUB - 1,)), dma((SUB - 1,)),
            dma((WIDE - 1,)), dma((WIDE,)),
            dma((SUB - 1,)), dma((SUB - 1,)),
            dma((SUB - 1,)), dma((SUB,)),
            dma((1,)), dma((1,)),
            dma((SUB // 2 - 1,)), dma((SUB // 2 - 1,)),
            dma((SUB - 1,)), dma((SUB - 1,)),
            dma((SUB // 2 - 1,)), dma((SUB // 2 - 1,)),
            dma((2,)), dma((2,)),
        ],
        compiler_params=pltpu.CompilerParams(
            collective_id=0, has_side_effects=True, vmem_limit_bytes=60 << 20
        ),
    )(
        krylov_basis.reshape(BASIS, ROWS, NODES),
        quad_weight,
        corrections.reshape(near_blocks, NODES, NODES),
        patch_route.reshape(1, PATCHES),
        leaf_slot.reshape(1, PATCHES),
        multipole_map,
        upward_translation,
        far_coupling.reshape(WIDE * SHARE, COEFFS),
        downward_translation,
        evaluation_map,
    )
    return vector.reshape(PATCHES, RHS, NODES), hessenberg


def solution(mesh):
    return jax.shard_map(
        per_device,
        mesh=mesh,
        in_specs=(
            P(None, ("wide", "sub"), None, None),
            P(("wide", "sub"), None),
            P(("wide", "sub"), None, None, None),
            P(("wide", "sub"), None),
            P(("wide", "sub")),
            P(),
            P(("wide", "sub"), None, None),
            P("wide", None, "sub", None),
            P(("wide", "sub"), None, None),
            P(),
        ),
        out_specs=(P(("wide", "sub"), None, None), P()),
        check_vma=False,
    )
```

```python
import functools

import jax
import jax.numpy as jnp
from jax import lax
from jax.experimental import pallas as pl
from jax.experimental.pallas import tpu as pltpu
from jax.sharding import PartitionSpec as P

MESH = pl.DeviceIdType.MESH
F32 = jnp.float32
BF16 = jnp.bfloat16
WIDE, SUB = 16, 8
PATCHES, RHS, NODES, COEFFS, BASIS, LEAVES = 128, 16, 128, 256, 4, 8
SHARE = COEFFS // SUB
ROWS = PATCHES * RHS
TOTAL = float(WIDE * SUB * PATCHES * NODES)
SCALE = 1.0 / 32.0
PACK = NODES // RHS
DEVICES = WIDE * SUB
PAIRS = [(j, k) for j in range(BASIS) for k in range(j, BASIS)]
NEAR_CHUNKS = 4


def split(value):
    high = value.astype(BF16)
    return high, (value - high.astype(F32)).astype(BF16)


def dot(a, b):
    return jnp.dot(a, b, preferred_element_type=F32)


def split_dot(value, high_ref, low_ref):
    high, low = split(value)
    rows = value.shape[0]
    both = dot(jnp.concatenate([high, low], axis=0), high_ref[...])
    return both[:rows] + both[rows:] + dot(high, low_ref[...])


def patch_rows(p):
    return pl.ds(pl.multiple_of(p * RHS, RHS), RHS)


def kernel(
    basis_hbm, weight_hbm, corr_hbm, route_hbm, slot_hbm, multi_hbm, up_hbm, far_hbm, down_hbm,
    eval_hbm, vector_out, hess_out,
    basis, weight, corr, route_v, slot_v, route_s, slot_s, multi, up, far, down, evalm, edge_corr,
    up_high, up_low, far_high, far_low, down_high, down_low, image,
    send1, recv1, sums1, send2, recv2, send3, recv3, send4, recv4, field,
    edge_send, edge_recv, send7, recv7, bulk_send, pair_recv, pair_sums, bulk_recv, bulk_sums, area_send, area_recv,
    load_sem, corr_sem, edge_s, edge_r, s1, r1, s2, r2, s3, r3, s4, r4, s5, r5, s7, r7,
    s8, r8, s9, r9, s10, r10, pair_s, pair_r, entered,
):
    w = lax.axis_index("wide")
    s = lax.axis_index("sub")
    me = w * SUB + s
    below = lax.rem(me + WIDE * SUB - 1, WIDE * SUB)
    above = lax.rem(me + 1, WIDE * SUB)
    below_id = (below // SUB, lax.rem(below, SUB))
    above_id = (above // SUB, lax.rem(above, SUB))
    subs = [lax.rem(s + d, SUB) for d in range(1, SUB)]
    core = lax.rem(s, 2)
    sibling = (w, s + 1 - 2 * core)
    columns_z = [(lax.rem(s // 2 + d, SUB // 2), d - 1) for d in range(1, SUB // 2)]
    wides = [lax.rem(w + d, WIDE) for d in range(1, WIDE)]
    wide_sources = [lax.rem(w + WIDE - d, WIDE) for d in range(1, WIDE)]

    barrier = pltpu.get_barrier_semaphore()
    side = 4
    x_line = [(lax.rem(w + side * d, WIDE), s) for d in range(1, side)]
    y_line = [(w // side * side + lax.rem(w + d, side), s) for d in range(1, side)]
    peers = [(w, t) for t in subs] + x_line + y_line + [below_id, above_id]
    for peer in peers:
        pl.semaphore_signal(barrier, inc=1, device_id=peer, device_id_type=MESH)

    last = BASIS - 1
    loads = {}

    def load(name, source, target):
        copy = pltpu.make_async_copy(source, target, load_sem.at[len(loads)])
        copy.start()
        loads[name] = copy

    load("current", basis_hbm.at[last], basis.at[last])
    load("weight", weight_hbm, weight)
    load("route_v", route_hbm, route_v)
    load("slot_v", slot_hbm, slot_v)
    load("multi", multi_hbm, multi)
    load("up", up_hbm, up)
    load("edge0", corr_hbm.at[0], edge_corr.at[0])
    load("edge1", corr_hbm.at[3 * PATCHES - 1], edge_corr.at[1])
    load("basis", basis_hbm.at[pl.ds(0, last)], basis.at[pl.ds(0, last)])
    load("route_s", route_hbm, route_s)
    load("slot_s", slot_hbm, slot_s)
    blocks = 3 * PATCHES // NEAR_CHUNKS
    corr_loads = []
    for c in range(NEAR_CHUNKS):
        copy = pltpu.make_async_copy(
            corr_hbm.at[pl.ds(c * blocks, blocks)], corr.at[pl.ds(c * blocks, blocks)], corr_sem.at[c]
        )
        copy.start()
        corr_loads.append(copy)
    load("far", far_hbm, far)
    load("eval", eval_hbm, evalm)
    load("down", down_hbm, down)

    def start_all(copies):
        for copy in copies:
            copy.start()
        return copies

    def remote(source, target, send_sem, recv_sem, device):
        return pltpu.make_async_remote_copy(
            src_ref=source, dst_ref=target, send_sem=send_sem, recv_sem=recv_sem,
            device_id=device, device_id_type=MESH,
        )

    for name in ("current", "weight", "route_v", "slot_v"):
        loads[name].wait()
    leaf_row = route_v[...] * LEAVES + slot_v[...]
    leaf_count = SUB * LEAVES
    hot = (
        lax.broadcasted_iota(jnp.int32, (leaf_count, PATCHES), 0)
        == jnp.broadcast_to(leaf_row, (leaf_count, PATCHES))
    ).astype(F32).astype(BF16)
    scaled_weight = weight[...] * SCALE

    def leaf_sums(read, store):
        for r in range(0, RHS, 2):
            pair = [(read(pl.ds(r + i, PATCHES, stride=RHS)) * scaled_weight).astype(BF16) for i in range(2)]
            sums = dot(hot, jnp.concatenate(pair, axis=1))
            for t in range(SUB):
                rows = slice(t * LEAVES, (t + 1) * LEAVES)
                tile = jnp.concatenate([sums[rows, :NODES], sums[rows, NODES:]], axis=0)
                store(t, slice(r * LEAVES, (r + 2) * LEAVES), tile.astype(BF16))

    def store1(t, rows, tile):
        send1[t, rows, :] = tile

    leaf_sums(lambda rows: basis[last, rows, :], store1)

    pl.semaphore_wait(barrier, len(peers))
    for peer in x_line:
        pl.semaphore_signal(entered, inc=1, device_id=peer, device_id_type=MESH)
    copies1 = start_all([
        remote(send1.at[t], recv1.at[d], s1.at[d], r1.at[d], (w, t)) for d, t in enumerate(subs)
    ])

    loads["edge0"].wait()
    loads["edge1"].wait()
    edge_send[0] = dot(basis[last, 0:RHS, :].astype(BF16), edge_corr[0])
    edge_send[1] = dot(basis[last, ROWS - RHS:, :].astype(BF16), edge_corr[1])
    edges = start_all([
        remote(edge_send.at[0], edge_recv.at[0], edge_s.at[0], edge_r.at[0], below_id),
        remote(edge_send.at[1], edge_recv.at[1], edge_s.at[1], edge_r.at[1], above_id),
    ])

    loads["multi"].wait()
    loads["up"].wait()

    def compose_up(leaf, carry):
        high, low = split(up[leaf])
        product = dot(multi[...], high) + dot(multi[...], low)
        rows = pl.ds(pl.multiple_of(leaf * NODES, NODES), NODES)
        up_high[rows, :], up_low[rows, :] = split(product)
        return carry

    lax.fori_loop(0, LEAVES, compose_up, 0)

    def half(p):
        return basis[last, patch_rows(p), :].astype(BF16)

    def near_pair(h, carry):
        p = 2 * h + 1
        left = jnp.concatenate([half(p), half(p + 1)], axis=1)
        right = jnp.concatenate(
            [
                jnp.concatenate([corr[3 * p + 1], corr[3 * p + 2]], axis=1),
                jnp.concatenate([corr[3 * p + 3], corr[3 * p + 4]], axis=1),
            ],
            axis=0,
        )
        both = dot(left, right)
        image[patch_rows(p), :] = both[:, :NODES] + dot(half(p - 1), corr[3 * p - 1])
        image[patch_rows(p + 1), :] = both[:, NODES:] + dot(half(p + 2), corr[3 * p + 6])
        return carry

    chunk = PATCHES // NEAR_CHUNKS // 2

    def near_chunk(c):
        corr_loads[c].wait()
        lax.fori_loop(max(0, c * chunk - 1), (c + 1) * chunk - 1, near_pair, 0, unroll=5 if c == 0 else 8)

    def bulk_store(j):
        def store(t, rows, tile):
            bulk_send[t % 2, t // 2, j, rows, :] = tile

        return store

    loads["basis"].wait()
    for j in range(last):
        leaf_sums(functools.partial(lambda k, rows: basis[k, rows, :], j), bulk_store(j))
    area_high, area_low = split(weight[...])
    areas = dot(hot, area_high) + dot(hot, area_low)
    for t in range(SUB):
        area_send[t] = areas[t * LEAVES:(t + 1) * LEAVES]
    early = pl.ds(0, last)
    pair_early = remote(
        bulk_send.at[1 - core, :, early], pair_recv.at[:, early], pair_s.at[0], pair_r.at[0], sibling
    )
    pair_early.start()
    near_chunk(0)
    near_chunk(1)

    for copy in copies1:
        copy.wait_recv()
    total = send1[s].astype(F32)
    for d in range(SUB - 1):
        total = total + recv1[d].astype(F32)
    sums1[...] = total
    lanes = jnp.concatenate(
        [sums1[pl.ds(leaf, RHS, stride=LEAVES), :] for leaf in range(LEAVES)], axis=1
    )
    tree = split_dot(lanes, up_high, up_low)
    low_rows = RHS // 2
    lane_low = lax.broadcasted_iota(jnp.int32, (low_rows, NODES), 1)
    for h in range(2):
        top = tree[:low_rows, h * NODES:(h + 1) * NODES]
        bottom = tree[low_rows:, h * NODES:(h + 1) * NODES]
        send2[2 * h] = jnp.where(lane_low < NODES // 2, top, pltpu.roll(bottom, NODES // 2, 1))
        send2[2 * h + 1] = jnp.where(lane_low < NODES // 2, pltpu.roll(top, NODES // 2, 1), bottom)
    copies2 = start_all([
        remote(send2.at[t // 2], recv2.at[d], s2.at[d], r2.at[d], (w, t)) for d, t in enumerate(subs)
    ])

    def pair_add(j):
        for t in range(SUB // 2):
            both = bulk_send[core, t, j].astype(F32) + pair_recv[t, j].astype(F32)
            pair_sums[t, j] = both.astype(BF16)

    pair_early.wait_recv()
    for j in range(last):
        pair_add(j)
    copies8 = start_all([
        remote(
            pair_sums.at[t, early], bulk_recv.at[d, early], s8.at[d], r8.at[d], (w, 2 * t + core)
        )
        for t, d in columns_z
    ] + [
        remote(area_send.at[t], area_recv.at[d], s9.at[d], r9.at[d], (w, t)) for d, t in enumerate(subs)
    ])

    loads["far"].wait()
    far_high[...], far_low[...] = split(far[...])
    near_chunk(2)
    near_chunk(3)
    for copy in edges:
        copy.wait()

    def current_half(p):
        return basis[last, p * RHS:(p + 1) * RHS, :].astype(BF16)

    from_below = jnp.where(me > 0, edge_recv[1], 0.0)
    from_above = jnp.where(me < WIDE * SUB - 1, edge_recv[0], 0.0)
    end = PATCHES - 1
    image[0:RHS, :] = (
        dot(current_half(0), corr[1]) + dot(current_half(1), corr[3]) + from_below
    )
    image[end * RHS:, :] = (
        dot(current_half(end), corr[3 * end + 1])
        + dot(current_half(end - 1), corr[3 * end - 1])
        + from_above
    )
    leaf_sums(lambda rows: image[rows, :], bulk_store(last))
    pair_late = remote(
        bulk_send.at[1 - core, :, last], pair_recv.at[:, last], pair_s.at[1], pair_r.at[1], sibling
    )
    pair_late.start()
    for copy in copies1:
        copy.wait_send()

    for copy in copies2:
        copy.wait_recv()
    half_tree = send2[s // 2]
    for d in range(SUB - 1):
        half_tree = half_tree + recv2[d]
    lane = lax.broadcasted_iota(jnp.int32, (RHS, NODES), 1)
    mine = jnp.where(lax.rem(lane_low // SHARE, 2) == core, half_tree, 0.0)
    turn = lax.rem(w, 2) - core
    placed = jnp.where(turn == 1, pltpu.roll(mine, SHARE, 1), mine)
    placed = jnp.where(turn == -1, pltpu.roll(mine, NODES - SHARE, 1), placed)
    send3[...] = placed
    pl.semaphore_wait(entered, len(x_line))
    copies3 = start_all([
        remote(send3, recv3.at[w], s3.at[d], r3.at[w], (v, s)) for d, v in enumerate(wides)
    ])
    recv3[w] = placed

    pair_late.wait_recv()
    pair_add(last)
    copies10 = start_all([
        remote(pair_sums.at[t, last], bulk_recv.at[d, last], s10.at[d], r10.at[d], (w, 2 * t + core))
        for t, d in columns_z
    ])

    loads["eval"].wait()
    loads["down"].wait()

    def compose_down(leaf, carry):
        high, low = split(down[leaf])
        product = dot(high, evalm[...]) + dot(low, evalm[...])
        columns = pl.ds(pl.multiple_of(leaf * NODES, NODES), NODES)
        down_high[:, columns], down_low[:, columns] = split(product)
        return carry

    lax.fori_loop(0, LEAVES, compose_down, 0)
    zero = jnp.zeros((RHS, NODES), F32)

    def node_weight(p):
        return jnp.broadcast_to(weight[pl.ds(p, 1), :], (RHS, NODES))

    def gram_body(p, sums):
        rows = patch_rows(p)
        vectors = [basis[j, rows, :] for j in range(BASIS)]
        weighted = [v * node_weight(p) for v in vectors]
        return tuple(a + weighted[j] * vectors[k] for a, (j, k) in zip(sums, PAIRS))

    gram = lax.fori_loop(0, PATCHES, gram_body, (zero,) * len(PAIRS), unroll=2)
    row = lax.broadcasted_iota(jnp.int32, (RHS, NODES), 0)
    spots = [(lane // RHS == m) & (lane % RHS == row) for m in range(PACK)]

    def pack(tiles, first, values):
        tiles = list(tiles)
        for i, value in enumerate(values, first):
            total = jnp.sum(value, axis=1, keepdims=True)
            tiles[i // PACK] = jnp.where(spots[i % PACK], total, tiles[i // PACK])
        return tiles

    packed = pack([zero, zero], BASIS + 1, gram)
    for copy in copies2:
        copy.wait_send()

    for d, v in enumerate(wide_sources):
        remote(send3, recv3.at[v], s3.at[d], r3.at[v], (v, s)).wait_recv()
    tiles = []
    for g in range(WIDE // 4):
        first = recv3[4 * g] + recv3[4 * g + 1]
        second = recv3[4 * g + 2] + recv3[4 * g + 3]
        top = jnp.where(lane_low < NODES // 2, first, pltpu.roll(second, NODES // 2, 1))
        bottom = jnp.where(lane_low < NODES // 2, pltpu.roll(first, NODES // 2, 1), second)
        tiles.append(jnp.concatenate([top, bottom], axis=0))
    lanes = jnp.concatenate(tiles, axis=1)
    send4[...] = split_dot(lanes, far_high, far_low)
    copies4 = start_all([
        remote(send4, recv4.at[d], s4.at[d], r4.at[d], (w, t)) for d, t in enumerate(subs)
    ])

    def near_products(p, sums):
        rows = patch_rows(p)
        value = image[rows, :]
        weighted = value * node_weight(p)
        return tuple(
            a + weighted * (basis[i, rows, :] if i < BASIS else value) for i, a in enumerate(sums)
        )

    products = lax.fori_loop(0, PATCHES, near_products, (zero,) * (BASIS + 1), unroll=2)
    for copy in copies3:
        copy.wait_send()
    for copy in copies8 + copies10:
        copy.wait_recv()
    for j in range(BASIS):
        total = pair_sums[s // 2, j].astype(F32)
        for d in range(SUB // 2 - 1):
            total = total + bulk_recv[d, j].astype(F32)
        bulk_sums[j] = total
    area = area_send[s]
    for d in range(SUB - 1):
        area = area + area_recv[d]

    for copy in copies4:
        copy.wait_recv()
    local = send4[...]
    for d in range(SUB - 1):
        local = local + recv4[d]
    potentials = split_dot(local, down_high, down_low).astype(BF16)
    far_sums = [zero] * (BASIS + 2)
    for leaf in range(LEAVES):
        field[s * LEAVES + leaf] = potentials[:, leaf * NODES:(leaf + 1) * NODES]
        value = potentials[:, leaf * NODES:(leaf + 1) * NODES].astype(F32)
        rows = pl.ds(leaf, RHS, stride=LEAVES)
        others = [bulk_sums[j, rows, :] for j in range(last)]
        others += [sums1[rows, :], bulk_sums[last, rows, :]]
        others += [value * jnp.broadcast_to(area[leaf:leaf + 1], (RHS, NODES))]
        far_sums = [a + value * b for a, b in zip(far_sums, others)]
    products = [products[j] + far_sums[j] * (1.0 / SCALE) for j in range(BASIS)] + [
        products[BASIS] + far_sums[BASIS] * (2.0 / SCALE) + far_sums[BASIS + 1]
    ]
    packed = pack(packed, 0, products)
    for a in range(2):
        send7[a:a + 1, :] = jnp.sum(packed[a], axis=0, keepdims=True)

    own = pl.ds(s * LEAVES, LEAVES)
    copies5 = start_all([
        remote(field.at[own], field.at[own], s5.at[d], r5.at[s], (w, t)) for d, t in enumerate(subs)
    ])

    def share(v, t):
        return remote(send7, recv7.at[me], s7.at[0], r7.at[0], (v, t))

    def share_wide(d, carry):
        v = lax.rem(w + d, WIDE)
        for e in range(SUB):
            share(v, lax.rem(s + e, SUB)).start()
        return carry

    lax.fori_loop(1, WIDE, share_wide, 0)
    for t in subs:
        share(w, t).start()
    recv7[me] = send7[...]
    for name in ("route_s", "slot_s"):
        loads[name].wait()
    for copy in copies4 + copies8 + copies10 + [pair_early, pair_late]:
        copy.wait_send()

    for d in range(1, SUB):
        t = lax.rem(s + SUB - d, SUB)
        block = field.at[pl.ds(t * LEAVES, LEAVES)]
        remote(block, block, s5.at[d - 1], r5.at[t], (w, t)).wait_recv()

    def add_far(p, carry):
        rows = patch_rows(p)
        leaf = route_s[0, p] * LEAVES + slot_s[0, p]
        image[rows, :] = image[rows, :] + field[leaf].astype(F32)
        return carry

    lax.fori_loop(0, PATCHES, add_far, 0, unroll=4)
    for copy in copies5:
        copy.wait_send()
    others = recv7.at[pl.ds(0, DEVICES - 1)]
    everyone = remote(others, others, s7.at[0], r7.at[0], sibling)
    everyone.wait_recv()
    totals = jnp.sum(recv7[...], axis=0) * (1.0 / TOTAL)
    wholes = [jnp.broadcast_to(totals[a:a + 1], (RHS, NODES)) for a in range(2)]

    def column(i):
        return jnp.sum(jnp.where(spots[i % PACK], wholes[i // PACK], 0.0), axis=1, keepdims=True)

    gram_of = {}
    for i, (j, k) in enumerate(PAIRS):
        gram_of[j, k] = gram_of[k, j] = column(BASIS + 1 + i)
    fields = [column(j) for j in range(BASIS)]
    first = [fields[j] + 0.5 * gram_of[j, last] for j in range(BASIS)]
    coeffs = []
    for j in range(BASIS):
        second = first[j]
        for k in range(BASIS):
            second = second - gram_of[j, k] * first[k]
        coeffs.append(first[j] + second)
    deltas = [coeffs[j] - 0.5 if j == last else coeffs[j] for j in range(BASIS)]
    square = column(BASIS)
    for j in range(BASIS):
        inner = -2.0 * fields[j]
        for k in range(BASIS):
            inner = inner + gram_of[j, k] * deltas[k]
        square = square + deltas[j] * inner
    beta = jnp.sqrt(jnp.maximum(square, 0.0) + 1e-6)
    inverse = jnp.broadcast_to(1.0 / beta, (RHS, NODES))
    factors = [jnp.broadcast_to(value, (RHS, NODES)) * inverse for value in deltas]

    def final_body(p, carry):
        rows = patch_rows(p)
        value = image[rows, :] * inverse
        for j in range(BASIS):
            value = value - factors[j] * basis[j, rows, :]
        vector_out[rows, :] = value
        return carry

    lax.fori_loop(0, PATCHES, final_body, 0, unroll=4)
    columns = coeffs + [beta]
    for i, value in enumerate(columns):
        flat = jnp.sum(jnp.where(row == lane, value, 0.0), axis=0, keepdims=True)
        hess_out[i:i + 1, :] = flat[:, :RHS]
    everyone.wait_send()


def per_device(
    krylov_basis, quad_weight, corrections, patch_route, leaf_slot, multipole_map,
    upward_translation, far_coupling, downward_translation, evaluation_map,
):
    outside = pl.BlockSpec(memory_space=pl.ANY)
    inside = pl.BlockSpec(memory_space=pltpu.VMEM)
    dma = pltpu.SemaphoreType.DMA
    near_blocks = 3 * PATCHES
    vector, hessenberg = pl.pallas_call(
        kernel,
        out_shape=(
            pltpu.VMEM((ROWS, NODES), F32),
            pltpu.VMEM((BASIS + 1, RHS), F32),
        ),
        in_specs=[outside] * 10,
        out_specs=(inside, inside),
        scratch_shapes=[
            pltpu.VMEM((BASIS, ROWS, NODES), F32),
            pltpu.VMEM((PATCHES, NODES), F32),
            pltpu.VMEM((near_blocks, NODES, NODES), BF16),
            pltpu.VMEM((1, PATCHES), jnp.int32),
            pltpu.VMEM((1, PATCHES), jnp.int32),
            pltpu.SMEM((1, PATCHES), jnp.int32),
            pltpu.SMEM((1, PATCHES), jnp.int32),
            pltpu.VMEM((NODES, COEFFS), BF16),
            pltpu.VMEM((LEAVES, COEFFS, COEFFS), F32),
            pltpu.VMEM((WIDE * SHARE, COEFFS), F32),
            pltpu.VMEM((LEAVES, COEFFS, COEFFS), F32),
            pltpu.VMEM((COEFFS, NODES), BF16),
            pltpu.VMEM((2, NODES, NODES), BF16),
            pltpu.VMEM((LEAVES * NODES, COEFFS), BF16),
            pltpu.VMEM((LEAVES * NODES, COEFFS), BF16),
            pltpu.VMEM((WIDE * SHARE, COEFFS), BF16),
            pltpu.VMEM((WIDE * SHARE, COEFFS), BF16),
            pltpu.VMEM((COEFFS, LEAVES * NODES), BF16),
            pltpu.VMEM((COEFFS, LEAVES * NODES), BF16),
            pltpu.VMEM((ROWS, NODES), F32),
            pltpu.VMEM((SUB, RHS * LEAVES, NODES), BF16),
            pltpu.VMEM((SUB - 1, RHS * LEAVES, NODES), BF16),
            pltpu.VMEM((RHS * LEAVES, NODES), F32),
            pltpu.VMEM((4, RHS // 2, NODES), F32),
            pltpu.VMEM((SUB - 1, RHS // 2, NODES), F32),
            pltpu.VMEM((RHS // 2, NODES), F32),
            pltpu.VMEM((WIDE, RHS // 2, NODES), F32),
            pltpu.VMEM((RHS, COEFFS), F32),
            pltpu.VMEM((SUB - 1, RHS, COEFFS), F32),
            pltpu.VMEM((SUB * LEAVES, RHS, NODES), BF16),
            pltpu.VMEM((2, RHS, NODES), F32),
            pltpu.VMEM((2, RHS, NODES), F32),
            pltpu.VMEM((2, NODES), F32),
            pltpu.VMEM((DEVICES, 2, NODES), F32),
            pltpu.VMEM((2, SUB // 2, BASIS, RHS * LEAVES, NODES), BF16),
            pltpu.VMEM((SUB // 2, BASIS, RHS * LEAVES, NODES), BF16),
            pltpu.VMEM((SUB // 2, BASIS, RHS * LEAVES, NODES), BF16),
            pltpu.VMEM((SUB // 2 - 1, BASIS, RHS * LEAVES, NODES), BF16),
            pltpu.VMEM((BASIS, RHS * LEAVES, NODES), F32),
            pltpu.VMEM((SUB, LEAVES, NODES), F32),
            pltpu.VMEM((SUB - 1, LEAVES, NODES), F32),
            dma((16,)), dma((NEAR_CHUNKS,)), dma((2,)), dma((2,)),
            dma((SUB - 1,)), dma((SUB - 1,)),
            dma((SUB - 1,)), dma((SUB - 1,)),
            dma((WIDE - 1,)), dma((WIDE,)),
            dma((SUB - 1,)), dma((SUB - 1,)),
            dma((SUB - 1,)), dma((SUB,)),
            dma((1,)), dma((1,)),
            dma((SUB // 2 - 1,)), dma((SUB // 2 - 1,)),
            dma((SUB - 1,)), dma((SUB - 1,)),
            dma((SUB // 2 - 1,)), dma((SUB // 2 - 1,)),
            dma((2,)), dma((2,)),
            pltpu.SemaphoreType.REGULAR,
        ],
        compiler_params=pltpu.CompilerParams(
            collective_id=0, has_side_effects=True, vmem_limit_bytes=60 << 20
        ),
    )(
        krylov_basis.reshape(BASIS, ROWS, NODES),
        quad_weight,
        corrections.reshape(near_blocks, NODES, NODES),
        patch_route.reshape(1, PATCHES),
        leaf_slot.reshape(1, PATCHES),
        multipole_map,
        upward_translation,
        far_coupling.reshape(WIDE * SHARE, COEFFS),
        downward_translation,
        evaluation_map,
    )
    return vector.reshape(PATCHES, RHS, NODES), hessenberg


def solution(mesh):
    return jax.shard_map(
        per_device,
        mesh=mesh,
        in_specs=(
            P(None, ("wide", "sub"), None, None),
            P(("wide", "sub"), None),
            P(("wide", "sub"), None, None, None),
            P(("wide", "sub"), None),
            P(("wide", "sub")),
            P(),
            P(("wide", "sub"), None, None),
            P("wide", None, "sub", None),
            P(("wide", "sub"), None, None),
            P(),
        ),
        out_specs=(P(("wide", "sub"), None, None), P()),
        check_vma=False,
    )
```

```python
import functools

import jax
import jax.numpy as jnp
from jax import lax
from jax.experimental import pallas as pl
from jax.experimental.pallas import tpu as pltpu
from jax.sharding import PartitionSpec as P

MESH = pl.DeviceIdType.MESH
F32 = jnp.float32
BF16 = jnp.bfloat16
WIDE, SUB = 16, 8
PATCHES, RHS, NODES, COEFFS, BASIS, LEAVES = 128, 16, 128, 256, 4, 8
SHARE = COEFFS // SUB
ROWS = PATCHES * RHS
TOTAL = float(WIDE * SUB * PATCHES * NODES)
SCALE = 1.0 / 32.0
PACK = NODES // RHS
DEVICES = WIDE * SUB
PAIRS = [(j, k) for j in range(BASIS) for k in range(j, BASIS)]
NEAR_CHUNKS = 4


def split(value):
    high = value.astype(BF16)
    return high, (value - high.astype(F32)).astype(BF16)


def dot(a, b):
    return jnp.dot(a, b, preferred_element_type=F32)


def split_dot(value, high_ref, low_ref):
    high, low = split(value)
    rows = value.shape[0]
    both = dot(jnp.concatenate([high, low], axis=0), high_ref[...])
    return both[:rows] + both[rows:] + dot(high, low_ref[...])


def patch_rows(p):
    return pl.ds(pl.multiple_of(p * RHS, RHS), RHS)


def kernel(
    basis_hbm, weight_hbm, corr_hbm, route_hbm, slot_hbm, multi_hbm, up_hbm, far_hbm, down_hbm,
    eval_hbm, vector_out, hess_out,
    basis, weight, corr, route_v, slot_v, route_s, slot_s, multi, up, far, down, evalm, edge_corr,
    up_high, up_low, far_high, far_low, down_high, down_low, image,
    send1, recv1, sums1, send2, recv2, send3, recv3, send4, recv4, field,
    edge_send, edge_recv, send7, recv7, bulk_send, pair_recv, pair_sums, bulk_recv, bulk_sums, area_send, area_recv,
    load_sem, corr_sem, edge_s, edge_r, s1, r1, s2, r2, s3, r3, s4, r4, s5, r5, s7, r7,
    s8, r8, s9, r9, s10, r10, pair_s, pair_r, entered,
):
    w = lax.axis_index("wide")
    s = lax.axis_index("sub")
    me = w * SUB + s
    below = lax.rem(me + WIDE * SUB - 1, WIDE * SUB)
    above = lax.rem(me + 1, WIDE * SUB)
    below_id = (below // SUB, lax.rem(below, SUB))
    above_id = (above // SUB, lax.rem(above, SUB))
    subs = [lax.rem(s + d, SUB) for d in range(1, SUB)]
    core = lax.rem(s, 2)
    sibling = (w, s + 1 - 2 * core)
    columns_z = [(lax.rem(s // 2 + d, SUB // 2), d - 1) for d in range(1, SUB // 2)]
    wides = [lax.rem(w + d, WIDE) for d in range(1, WIDE)]
    wide_sources = [lax.rem(w + WIDE - d, WIDE) for d in range(1, WIDE)]

    barrier = pltpu.get_barrier_semaphore()
    side = 4
    x_line = [(lax.rem(w + side * d, WIDE), s) for d in range(1, side)]
    y_line = [(w // side * side + lax.rem(w + d, side), s) for d in range(1, side)]
    peers = [(w, t) for t in subs] + x_line + y_line + [below_id, above_id]
    for peer in peers:
        pl.semaphore_signal(barrier, inc=1, device_id=peer, device_id_type=MESH)

    last = BASIS - 1
    loads = {}

    def load(name, source, target):
        copy = pltpu.make_async_copy(source, target, load_sem.at[len(loads)])
        copy.start()
        loads[name] = copy

    load("current", basis_hbm.at[last], basis.at[last])
    load("weight", weight_hbm, weight)
    load("route_v", route_hbm, route_v)
    load("slot_v", slot_hbm, slot_v)
    load("multi", multi_hbm, multi)
    load("up", up_hbm, up)
    load("edge0", corr_hbm.at[0], edge_corr.at[0])
    load("edge1", corr_hbm.at[3 * PATCHES - 1], edge_corr.at[1])
    load("basis", basis_hbm.at[pl.ds(0, last)], basis.at[pl.ds(0, last)])
    load("route_s", route_hbm, route_s)
    load("slot_s", slot_hbm, slot_s)
    blocks = 3 * PATCHES // NEAR_CHUNKS
    corr_loads = []
    for c in range(NEAR_CHUNKS):
        copy = pltpu.make_async_copy(
            corr_hbm.at[pl.ds(c * blocks, blocks)], corr.at[pl.ds(c * blocks, blocks)], corr_sem.at[c]
        )
        copy.start()
        corr_loads.append(copy)
    load("far", far_hbm, far)
    load("eval", eval_hbm, evalm)
    load("down", down_hbm, down)

    def start_all(copies):
        for copy in copies:
            copy.start()
        return copies

    def remote(source, target, send_sem, recv_sem, device):
        return pltpu.make_async_remote_copy(
            src_ref=source, dst_ref=target, send_sem=send_sem, recv_sem=recv_sem,
            device_id=device, device_id_type=MESH,
        )

    for name in ("current", "weight", "route_v", "slot_v"):
        loads[name].wait()
    leaf_row = route_v[...] * LEAVES + slot_v[...]
    leaf_count = SUB * LEAVES
    hot = (
        lax.broadcasted_iota(jnp.int32, (leaf_count, PATCHES), 0)
        == jnp.broadcast_to(leaf_row, (leaf_count, PATCHES))
    ).astype(F32).astype(BF16)
    scaled_weight = weight[...] * SCALE

    def leaf_sums(read, store):
        for r in range(0, RHS, 2):
            pair = [(read(pl.ds(r + i, PATCHES, stride=RHS)) * scaled_weight).astype(BF16) for i in range(2)]
            sums = dot(hot, jnp.concatenate(pair, axis=1))
            for t in range(SUB):
                rows = slice(t * LEAVES, (t + 1) * LEAVES)
                tile = jnp.concatenate([sums[rows, :NODES], sums[rows, NODES:]], axis=0)
                store(t, slice(r * LEAVES, (r + 2) * LEAVES), tile.astype(BF16))

    def store1(t, rows, tile):
        send1[t, rows, :] = tile

    leaf_sums(lambda rows: basis[last, rows, :], store1)

    pl.semaphore_wait(barrier, len(peers))
    for peer in x_line:
        pl.semaphore_signal(entered, inc=1, device_id=peer, device_id_type=MESH)
    copies1 = start_all([
        remote(send1.at[t], recv1.at[d], s1.at[d], r1.at[d], (w, t)) for d, t in enumerate(subs)
    ])

    loads["edge0"].wait()
    loads["edge1"].wait()
    edge_send[0] = dot(basis[last, 0:RHS, :].astype(BF16), edge_corr[0])
    edge_send[1] = dot(basis[last, ROWS - RHS:, :].astype(BF16), edge_corr[1])
    edges = start_all([
        remote(edge_send.at[0], edge_recv.at[0], edge_s.at[0], edge_r.at[0], below_id),
        remote(edge_send.at[1], edge_recv.at[1], edge_s.at[1], edge_r.at[1], above_id),
    ])

    loads["multi"].wait()
    loads["up"].wait()

    def compose_up(leaf, carry):
        high, low = split(up[leaf])
        product = dot(multi[...], high) + dot(multi[...], low)
        rows = pl.ds(pl.multiple_of(leaf * NODES, NODES), NODES)
        up_high[rows, :], up_low[rows, :] = split(product)
        return carry

    lax.fori_loop(0, LEAVES, compose_up, 0)

    def half(p):
        return basis[last, patch_rows(p), :].astype(BF16)

    def near_pair(h, carry):
        p = 2 * h + 1
        left = jnp.concatenate([half(p), half(p + 1)], axis=1)
        right = jnp.concatenate(
            [
                jnp.concatenate([corr[3 * p + 1], corr[3 * p + 2]], axis=1),
                jnp.concatenate([corr[3 * p + 3], corr[3 * p + 4]], axis=1),
            ],
            axis=0,
        )
        both = dot(left, right)
        image[patch_rows(p), :] = both[:, :NODES] + dot(half(p - 1), corr[3 * p - 1])
        image[patch_rows(p + 1), :] = both[:, NODES:] + dot(half(p + 2), corr[3 * p + 6])
        return carry

    chunk = PATCHES // NEAR_CHUNKS // 2

    def near_chunk(c):
        corr_loads[c].wait()
        lax.fori_loop(max(0, c * chunk - 1), (c + 1) * chunk - 1, near_pair, 0, unroll=5 if c == 0 else 8)

    def bulk_store(j):
        def store(t, rows, tile):
            bulk_send[t % 2, t // 2, j, rows, :] = tile

        return store

    loads["basis"].wait()
    for j in range(last):
        leaf_sums(functools.partial(lambda k, rows: basis[k, rows, :], j), bulk_store(j))
    area_high, area_low = split(weight[...])
    areas = dot(hot, area_high) + dot(hot, area_low)
    for t in range(SUB):
        area_send[t] = areas[t * LEAVES:(t + 1) * LEAVES]
    early = pl.ds(0, last)
    pair_early = remote(
        bulk_send.at[1 - core, :, early], pair_recv.at[:, early], pair_s.at[0], pair_r.at[0], sibling
    )
    pair_early.start()
    near_chunk(0)
    near_chunk(1)

    for copy in copies1:
        copy.wait_recv()
    total = send1[s].astype(F32)
    for d in range(SUB - 1):
        total = total + recv1[d].astype(F32)
    sums1[...] = total
    lanes = jnp.concatenate(
        [sums1[pl.ds(leaf, RHS, stride=LEAVES), :] for leaf in range(LEAVES)], axis=1
    )
    tree = split_dot(lanes, up_high, up_low)
    low_rows = RHS // 2
    lane_low = lax.broadcasted_iota(jnp.int32, (low_rows, NODES), 1)
    for h in range(2):
        top = tree[:low_rows, h * NODES:(h + 1) * NODES]
        bottom = tree[low_rows:, h * NODES:(h + 1) * NODES]
        send2[2 * h] = jnp.where(lane_low < NODES // 2, top, pltpu.roll(bottom, NODES // 2, 1))
        send2[2 * h + 1] = jnp.where(lane_low < NODES // 2, pltpu.roll(top, NODES // 2, 1), bottom)
    copies2 = start_all([
        remote(send2.at[t // 2], recv2.at[d], s2.at[d], r2.at[d], (w, t)) for d, t in enumerate(subs)
    ])

    def pair_add(j):
        for t in range(SUB // 2):
            both = bulk_send[core, t, j].astype(F32) + pair_recv[t, j].astype(F32)
            pair_sums[t, j] = both.astype(BF16)

    pair_early.wait_recv()
    for j in range(last):
        pair_add(j)
    copies8 = start_all([
        remote(
            pair_sums.at[t, early], bulk_recv.at[d, early], s8.at[d], r8.at[d], (w, 2 * t + core)
        )
        for t, d in columns_z
    ])

    loads["far"].wait()
    far_high[...], far_low[...] = split(far[...])
    near_chunk(2)
    near_chunk(3)
    for copy in edges:
        copy.wait()

    def current_half(p):
        return basis[last, p * RHS:(p + 1) * RHS, :].astype(BF16)

    from_below = jnp.where(me > 0, edge_recv[1], 0.0)
    from_above = jnp.where(me < WIDE * SUB - 1, edge_recv[0], 0.0)
    end = PATCHES - 1
    image[0:RHS, :] = (
        dot(current_half(0), corr[1]) + dot(current_half(1), corr[3]) + from_below
    )
    image[end * RHS:, :] = (
        dot(current_half(end), corr[3 * end + 1])
        + dot(current_half(end - 1), corr[3 * end - 1])
        + from_above
    )
    leaf_sums(lambda rows: image[rows, :], bulk_store(last))
    pair_late = remote(
        bulk_send.at[1 - core, :, last], pair_recv.at[:, last], pair_s.at[1], pair_r.at[1], sibling
    )
    pair_late.start()
    for copy in copies1:
        copy.wait_send()

    for copy in copies2:
        copy.wait_recv()
    half_tree = send2[s // 2]
    for d in range(SUB - 1):
        half_tree = half_tree + recv2[d]
    lane = lax.broadcasted_iota(jnp.int32, (RHS, NODES), 1)
    mine = jnp.where(lax.rem(lane_low // SHARE, 2) == core, half_tree, 0.0)
    turn = lax.rem(w, 2) - core
    placed = jnp.where(turn == 1, pltpu.roll(mine, SHARE, 1), mine)
    placed = jnp.where(turn == -1, pltpu.roll(mine, NODES - SHARE, 1), placed)
    send3[...] = placed
    pl.semaphore_wait(entered, len(x_line))
    copies3 = start_all([
        remote(send3, recv3.at[w], s3.at[d], r3.at[w], (v, s)) for d, v in enumerate(wides)
    ])
    recv3[w] = placed

    pair_late.wait_recv()
    pair_add(last)
    copies10 = start_all([
        remote(pair_sums.at[t, last], bulk_recv.at[d, last], s10.at[d], r10.at[d], (w, 2 * t + core))
        for t, d in columns_z
    ] + [
        remote(area_send.at[t], area_recv.at[d], s9.at[d], r9.at[d], (w, t)) for d, t in enumerate(subs)
    ])

    loads["eval"].wait()
    loads["down"].wait()

    def compose_down(leaf, carry):
        high, low = split(down[leaf])
        product = dot(high, evalm[...]) + dot(low, evalm[...])
        columns = pl.ds(pl.multiple_of(leaf * NODES, NODES), NODES)
        down_high[:, columns], down_low[:, columns] = split(product)
        return carry

    lax.fori_loop(0, LEAVES, compose_down, 0)
    zero = jnp.zeros((RHS, NODES), F32)

    def node_weight(p):
        return jnp.broadcast_to(weight[pl.ds(p, 1), :], (RHS, NODES))

    def gram_body(p, sums):
        rows = patch_rows(p)
        vectors = [basis[j, rows, :] for j in range(BASIS)]
        weighted = [v * node_weight(p) for v in vectors]
        return tuple(a + weighted[j] * vectors[k] for a, (j, k) in zip(sums, PAIRS))

    gram = lax.fori_loop(0, PATCHES, gram_body, (zero,) * len(PAIRS), unroll=2)
    row = lax.broadcasted_iota(jnp.int32, (RHS, NODES), 0)
    spots = [(lane // RHS == m) & (lane % RHS == row) for m in range(PACK)]

    def pack(tiles, first, values):
        tiles = list(tiles)
        for i, value in enumerate(values, first):
            total = jnp.sum(value, axis=1, keepdims=True)
            tiles[i // PACK] = jnp.where(spots[i % PACK], total, tiles[i // PACK])
        return tiles

    packed = pack([zero, zero], BASIS + 1, gram)
    for copy in copies2:
        copy.wait_send()

    for d, v in enumerate(wide_sources):
        remote(send3, recv3.at[v], s3.at[d], r3.at[v], (v, s)).wait_recv()
    tiles = []
    for g in range(WIDE // 4):
        first = recv3[4 * g] + recv3[4 * g + 1]
        second = recv3[4 * g + 2] + recv3[4 * g + 3]
        top = jnp.where(lane_low < NODES // 2, first, pltpu.roll(second, NODES // 2, 1))
        bottom = jnp.where(lane_low < NODES // 2, pltpu.roll(first, NODES // 2, 1), second)
        tiles.append(jnp.concatenate([top, bottom], axis=0))
    lanes = jnp.concatenate(tiles, axis=1)
    send4[...] = split_dot(lanes, far_high, far_low)
    copies4 = start_all([
        remote(send4, recv4.at[d], s4.at[d], r4.at[d], (w, t)) for d, t in enumerate(subs)
    ])

    def near_products(p, sums):
        rows = patch_rows(p)
        value = image[rows, :]
        weighted = value * node_weight(p)
        return tuple(
            a + weighted * (basis[i, rows, :] if i < BASIS else value) for i, a in enumerate(sums)
        )

    products = lax.fori_loop(0, PATCHES, near_products, (zero,) * (BASIS + 1), unroll=2)
    for copy in copies3:
        copy.wait_send()
    for copy in copies8 + copies10:
        copy.wait_recv()
    for j in range(BASIS):
        total = pair_sums[s // 2, j].astype(F32)
        for d in range(SUB // 2 - 1):
            total = total + bulk_recv[d, j].astype(F32)
        bulk_sums[j] = total
    area = area_send[s]
    for d in range(SUB - 1):
        area = area + area_recv[d]

    for copy in copies4:
        copy.wait_recv()
    local = send4[...]
    for d in range(SUB - 1):
        local = local + recv4[d]
    potentials = split_dot(local, down_high, down_low).astype(BF16)
    far_sums = [zero] * (BASIS + 2)
    for leaf in range(LEAVES):
        field[s * LEAVES + leaf] = potentials[:, leaf * NODES:(leaf + 1) * NODES]
        value = potentials[:, leaf * NODES:(leaf + 1) * NODES].astype(F32)
        rows = pl.ds(leaf, RHS, stride=LEAVES)
        others = [bulk_sums[j, rows, :] for j in range(last)]
        others += [sums1[rows, :], bulk_sums[last, rows, :]]
        others += [value * jnp.broadcast_to(area[leaf:leaf + 1], (RHS, NODES))]
        far_sums = [a + value * b for a, b in zip(far_sums, others)]
    products = [products[j] + far_sums[j] * (1.0 / SCALE) for j in range(BASIS)] + [
        products[BASIS] + far_sums[BASIS] * (2.0 / SCALE) + far_sums[BASIS + 1]
    ]
    packed = pack(packed, 0, products)
    for a in range(2):
        send7[a:a + 1, :] = jnp.sum(packed[a], axis=0, keepdims=True)

    own = pl.ds(s * LEAVES, LEAVES)
    copies5 = start_all([
        remote(field.at[own], field.at[own], s5.at[d], r5.at[s], (w, t)) for d, t in enumerate(subs)
    ])

    def share(v, t):
        return remote(send7, recv7.at[me], s7.at[0], r7.at[0], (v, t))

    def share_wide(d, carry):
        v = lax.rem(w + d, WIDE)
        for e in range(SUB):
            share(v, lax.rem(s + e, SUB)).start()
        return carry

    lax.fori_loop(1, WIDE, share_wide, 0)
    for t in subs:
        share(w, t).start()
    recv7[me] = send7[...]
    for name in ("route_s", "slot_s"):
        loads[name].wait()
    for copy in copies4 + copies8 + copies10 + [pair_early, pair_late]:
        copy.wait_send()

    for d in range(1, SUB):
        t = lax.rem(s + SUB - d, SUB)
        block = field.at[pl.ds(t * LEAVES, LEAVES)]
        remote(block, block, s5.at[d - 1], r5.at[t], (w, t)).wait_recv()

    def add_far(p, carry):
        rows = patch_rows(p)
        leaf = route_s[0, p] * LEAVES + slot_s[0, p]
        image[rows, :] = image[rows, :] + field[leaf].astype(F32)
        return carry

    lax.fori_loop(0, PATCHES, add_far, 0, unroll=4)
    for copy in copies5:
        copy.wait_send()
    others = recv7.at[pl.ds(0, DEVICES - 1)]
    everyone = remote(others, others, s7.at[0], r7.at[0], sibling)
    everyone.wait_recv()
    totals = jnp.sum(recv7[...], axis=0) * (1.0 / TOTAL)
    wholes = [jnp.broadcast_to(totals[a:a + 1], (RHS, NODES)) for a in range(2)]

    def column(i):
        return jnp.sum(jnp.where(spots[i % PACK], wholes[i // PACK], 0.0), axis=1, keepdims=True)

    gram_of = {}
    for i, (j, k) in enumerate(PAIRS):
        gram_of[j, k] = gram_of[k, j] = column(BASIS + 1 + i)
    fields = [column(j) for j in range(BASIS)]
    first = [fields[j] + 0.5 * gram_of[j, last] for j in range(BASIS)]
    coeffs = []
    for j in range(BASIS):
        second = first[j]
        for k in range(BASIS):
            second = second - gram_of[j, k] * first[k]
        coeffs.append(first[j] + second)
    deltas = [coeffs[j] - 0.5 if j == last else coeffs[j] for j in range(BASIS)]
    square = column(BASIS)
    for j in range(BASIS):
        inner = -2.0 * fields[j]
        for k in range(BASIS):
            inner = inner + gram_of[j, k] * deltas[k]
        square = square + deltas[j] * inner
    beta = jnp.sqrt(jnp.maximum(square, 0.0) + 1e-6)
    inverse = jnp.broadcast_to(1.0 / beta, (RHS, NODES))
    factors = [jnp.broadcast_to(value, (RHS, NODES)) * inverse for value in deltas]

    def final_body(p, carry):
        rows = patch_rows(p)
        value = image[rows, :] * inverse
        for j in range(BASIS):
            value = value - factors[j] * basis[j, rows, :]
        vector_out[rows, :] = value
        return carry

    lax.fori_loop(0, PATCHES, final_body, 0, unroll=4)
    columns = coeffs + [beta]
    for i, value in enumerate(columns):
        flat = jnp.sum(jnp.where(row == lane, value, 0.0), axis=0, keepdims=True)
        hess_out[i:i + 1, :] = flat[:, :RHS]
    everyone.wait_send()


def per_device(
    krylov_basis, quad_weight, corrections, patch_route, leaf_slot, multipole_map,
    upward_translation, far_coupling, downward_translation, evaluation_map,
):
    outside = pl.BlockSpec(memory_space=pl.ANY)
    inside = pl.BlockSpec(memory_space=pltpu.VMEM)
    dma = pltpu.SemaphoreType.DMA
    near_blocks = 3 * PATCHES
    vector, hessenberg = pl.pallas_call(
        kernel,
        out_shape=(
            pltpu.VMEM((ROWS, NODES), F32),
            pltpu.VMEM((BASIS + 1, RHS), F32),
        ),
        in_specs=[outside] * 10,
        out_specs=(inside, inside),
        scratch_shapes=[
            pltpu.VMEM((BASIS, ROWS, NODES), F32),
            pltpu.VMEM((PATCHES, NODES), F32),
            pltpu.VMEM((near_blocks, NODES, NODES), BF16),
            pltpu.VMEM((1, PATCHES), jnp.int32),
            pltpu.VMEM((1, PATCHES), jnp.int32),
            pltpu.SMEM((1, PATCHES), jnp.int32),
            pltpu.SMEM((1, PATCHES), jnp.int32),
            pltpu.VMEM((NODES, COEFFS), BF16),
            pltpu.VMEM((LEAVES, COEFFS, COEFFS), F32),
            pltpu.VMEM((WIDE * SHARE, COEFFS), F32),
            pltpu.VMEM((LEAVES, COEFFS, COEFFS), F32),
            pltpu.VMEM((COEFFS, NODES), BF16),
            pltpu.VMEM((2, NODES, NODES), BF16),
            pltpu.VMEM((LEAVES * NODES, COEFFS), BF16),
            pltpu.VMEM((LEAVES * NODES, COEFFS), BF16),
            pltpu.VMEM((WIDE * SHARE, COEFFS), BF16),
            pltpu.VMEM((WIDE * SHARE, COEFFS), BF16),
            pltpu.VMEM((COEFFS, LEAVES * NODES), BF16),
            pltpu.VMEM((COEFFS, LEAVES * NODES), BF16),
            pltpu.VMEM((ROWS, NODES), F32),
            pltpu.VMEM((SUB, RHS * LEAVES, NODES), BF16),
            pltpu.VMEM((SUB - 1, RHS * LEAVES, NODES), BF16),
            pltpu.VMEM((RHS * LEAVES, NODES), F32),
            pltpu.VMEM((4, RHS // 2, NODES), F32),
            pltpu.VMEM((SUB - 1, RHS // 2, NODES), F32),
            pltpu.VMEM((RHS // 2, NODES), F32),
            pltpu.VMEM((WIDE, RHS // 2, NODES), F32),
            pltpu.VMEM((RHS, COEFFS), F32),
            pltpu.VMEM((SUB - 1, RHS, COEFFS), F32),
            pltpu.VMEM((SUB * LEAVES, RHS, NODES), BF16),
            pltpu.VMEM((2, RHS, NODES), F32),
            pltpu.VMEM((2, RHS, NODES), F32),
            pltpu.VMEM((2, NODES), F32),
            pltpu.VMEM((DEVICES, 2, NODES), F32),
            pltpu.VMEM((2, SUB // 2, BASIS, RHS * LEAVES, NODES), BF16),
            pltpu.VMEM((SUB // 2, BASIS, RHS * LEAVES, NODES), BF16),
            pltpu.VMEM((SUB // 2, BASIS, RHS * LEAVES, NODES), BF16),
            pltpu.VMEM((SUB // 2 - 1, BASIS, RHS * LEAVES, NODES), BF16),
            pltpu.VMEM((BASIS, RHS * LEAVES, NODES), F32),
            pltpu.VMEM((SUB, LEAVES, NODES), F32),
            pltpu.VMEM((SUB - 1, LEAVES, NODES), F32),
            dma((16,)), dma((NEAR_CHUNKS,)), dma((2,)), dma((2,)),
            dma((SUB - 1,)), dma((SUB - 1,)),
            dma((SUB - 1,)), dma((SUB - 1,)),
            dma((WIDE - 1,)), dma((WIDE,)),
            dma((SUB - 1,)), dma((SUB - 1,)),
            dma((SUB - 1,)), dma((SUB,)),
            dma((1,)), dma((1,)),
            dma((SUB // 2 - 1,)), dma((SUB // 2 - 1,)),
            dma((SUB - 1,)), dma((SUB - 1,)),
            dma((SUB // 2 - 1,)), dma((SUB // 2 - 1,)),
            dma((2,)), dma((2,)),
            pltpu.SemaphoreType.REGULAR,
        ],
        compiler_params=pltpu.CompilerParams(
            collective_id=0, has_side_effects=True, vmem_limit_bytes=60 << 20
        ),
    )(
        krylov_basis.reshape(BASIS, ROWS, NODES),
        quad_weight,
        corrections.reshape(near_blocks, NODES, NODES),
        patch_route.reshape(1, PATCHES),
        leaf_slot.reshape(1, PATCHES),
        multipole_map,
        upward_translation,
        far_coupling.reshape(WIDE * SHARE, COEFFS),
        downward_translation,
        evaluation_map,
    )
    return vector.reshape(PATCHES, RHS, NODES), hessenberg


def solution(mesh):
    return jax.shard_map(
        per_device,
        mesh=mesh,
        in_specs=(
            P(None, ("wide", "sub"), None, None),
            P(("wide", "sub"), None),
            P(("wide", "sub"), None, None, None),
            P(("wide", "sub"), None),
            P(("wide", "sub")),
            P(),
            P(("wide", "sub"), None, None),
            P("wide", None, "sub", None),
            P(("wide", "sub"), None, None),
            P(),
        ),
        out_specs=(P(("wide", "sub"), None, None), P()),
        check_vma=False,
    )
```
